32 devices in a mesh: ph: 4 (over x, core), ka: 8 (over z, y).
Axes of the slice: x: 2, y: 2, z: 4, core: 2. Of those that a mesh axis runs over, the one named last changes fastest.
Arguments:
- g_wan: bfloat16 [32, 48, 48, 2, 1024], P('ka', 'ph'), may hold values from -6 to 6
- el_cells: int32 [3, 32], replicated, may hold values from -6 to 6
- ph_cells: int32 [3, 48], P(None, 'ph'), may hold values from -4 to 4
- q_point: int32 [3], replicated, may hold values from 0 to 63
- kpoints: int32 [3, 2048], P(None, 'ka'), may hold values from 0 to 63
- eigvec: float32 [2, 48, 48], replicated, may hold values from -0.875 to 0.875
- omega: float32 [48], replicated, may hold values from 0.25 to 4
Outputs:
- strength: float32 [48, 32, 2048], P('ph', None, 'ka')
The draws below stay inside these ranges and needn't reach their ends.
All inputs are finite; a program needn't handle non-finite values.
Results may differ from the reference program's by a relative error of at most 0.0018.
Values may be sent and summed in bfloat16 or wider, within the bound.
A program may use at most 128 MiB of HBM per device.

```python
import math
import jax
import jax.numpy as jnp
from jax import lax

W = 32
NU = 48
KGRID = 64
K_DEV = 256
NRE = 32
NRP = 48
NK = 2048
N_KA = 8


def place_ends(array, key, low, high):
    dims = array.shape
    index_at = [jax.random.randint(jax.random.fold_in(key, axis), (), 0, dims[axis]) for axis in range(len(dims))]
    array = array.at[tuple(index_at)].set(low)
    longest = dims.index(max(dims))
    index_at[longest] = (index_at[longest] + 1) % dims[longest]
    return array.at[tuple(index_at)].set(high)


def shard_levels(key, dims, shards, low, high):
    loudness, own = 1.0, jax.random.fold_in(key, 6)
    for dim, parts in shards:
        heights = jnp.exp(jax.random.uniform(jax.random.fold_in(own, dim), (parts,), jnp.float32, low / len(shards), high / len(shards)))
        loudness = loudness * jnp.repeat(heights, dims[dim] // parts).reshape([-1 if axis == dim else 1 for axis in range(len(dims))])
    return loudness


def scatter_about(stream_key, extent, width, most, split=(), held_as=jnp.bfloat16):
    loudness = shard_levels(stream_key, extent, split, -0.22, 0.18) if split else 1.0
    result = jax.random.normal(stream_key, extent, jnp.float32) * width * loudness
    return jnp.minimum(jnp.maximum(result, -most), most).astype(held_as)


def setup_inputs(seed: int = 0) -> dict:
    arg_keys = jax.random.split(jax.random.key(seed), 8)
    return {
        "g_wan": scatter_about(arg_keys[0], (NRE, NRP, NU, 2, W * W), 1.0, 6.0, ((0, 8), (1, 4))),
        "el_cells": place_ends(jax.random.randint(arg_keys[1], (3, NRE), -6, 7), jax.random.fold_in(arg_keys[1], 1), -6, 6).astype(jnp.int32),
        "ph_cells": place_ends(jax.random.randint(arg_keys[2], (3, NRP), -4, 5), jax.random.fold_in(arg_keys[2], 1), -4, 4).astype(jnp.int32),
        "q_point": jax.random.randint(arg_keys[3], (3,), 0, KGRID).astype(jnp.int32),
        "kpoints": place_ends(jax.random.randint(arg_keys[4], (3, NK), 0, KGRID), jax.random.fold_in(arg_keys[4], 1), 0, KGRID - 1).astype(jnp.int32),
        "eigvec": scatter_about(arg_keys[5], (2, NU, NU), NU ** -0.5, 0.875, (), jnp.float32),
        "omega": jnp.clip(jnp.exp(jax.random.uniform(arg_keys[6], (NU,), jnp.float32, math.log(0.25), math.log(4.0))), 0.25, 4.0),
    }


def angles(numerators, vectors):
    summed = lax.optimization_barrier(jnp.sum(numerators[:, :, None] * vectors[:, None, :], axis=0))
    return jnp.mod(summed, KGRID).astype(jnp.float32) * (2.0 * math.pi / KGRID)

def coupling(q_angle, eigvec, omega):
    mode_scale = 1.0 / jnp.sqrt(2.0 * omega)
    cos_phase = jnp.cos(q_angle)[:, None, None]
    sin_phase = jnp.sin(q_angle)[:, None, None]
    real_part = eigvec[0][None]
    imag_part = eigvec[1][None]
    coef_re = ((cos_phase * real_part - sin_phase * imag_part) * mode_scale).astype(jnp.bfloat16)
    coef_im = ((sin_phase * real_part + cos_phase * imag_part) * mode_scale).astype(jnp.bfloat16)
    return jnp.stack([jnp.stack([coef_re, coef_im], 2), jnp.stack([-coef_im, coef_re], 2)], 2)

def stacked(mode_block):
    row_count = mode_block.shape[0]
    vert_re = mode_block[:, :, 0, :].reshape(row_count, -1)
    vert_im = mode_block[:, :, 1, :].reshape(row_count, -1)
    upper = jnp.concatenate([vert_re, vert_im], 1)
    lower = jnp.concatenate([-vert_im, vert_re], 1)
    return jnp.concatenate([upper, lower], 0)

def pair_strength(bloch_sum, mode_count, normalizer):
    k_count = bloch_sum.shape[0]
    half_width = bloch_sum.shape[1] // 2
    bloch_re = bloch_sum[:, :half_width].reshape(k_count, mode_count, W, W)
    bloch_im = bloch_sum[:, half_width:].reshape(k_count, mode_count, W, W)
    summed = lax.optimization_barrier(jnp.sum(bloch_re * bloch_re + bloch_im * bloch_im, axis=3)) / normalizer
    return summed.transpose(1, 2, 0)

def reference(g_wan, el_cells, ph_cells, q_point, kpoints, eigvec, omega):
    q_angle = angles(q_point[:, None], ph_cells)[0]
    coupling_table = coupling(q_angle, eigvec, omega).astype(jnp.float32)

    def vertex_row(cell_row):
        return jnp.einsum('pncom,pncw->mow', coupling_table, cell_row.astype(jnp.float32))
    mode_vertex = lax.map(vertex_row, g_wan).astype(jnp.bfloat16)
    stacked_rows = stacked(mode_vertex)
    normalizer = float(NRE * NRP * W)
    k_blocks = kpoints.reshape(3, N_KA, K_DEV).transpose(1, 0, 2)

    def strength_block(k_numer):
        k_angle = angles(k_numer, el_cells)
        phase_left = jnp.concatenate([jnp.cos(k_angle), jnp.sin(k_angle)], 1).astype(jnp.bfloat16)
        bloch_sum = jnp.dot(phase_left, stacked_rows, preferred_element_type=jnp.float32)
        return pair_strength(bloch_sum, NU, normalizer)
    results = lax.map(strength_block, k_blocks)
    return results.transpose(1, 2, 0, 3).reshape(NU, W, NK)
```

```python
import functools
import math

import jax
import jax.numpy as jnp
from jax import lax
from jax.experimental import pallas as pl
from jax.experimental.pallas import tpu as pltpu
from jax.sharding import PartitionSpec as P

W = 32
KGRID = 64
MESH = pl.DeviceIdType.MESH


def angles(numerators, vectors):
    summed = jnp.sum(numerators[:, :, None] * vectors[:, None, :], axis=0)
    return jnp.mod(summed, KGRID).astype(jnp.float32) * (2.0 * math.pi / KGRID)


def splits(ways, width):
    by_width = math.gcd(ways, width // W)
    return by_width, ways // by_width


def coupling(q_angle, eigvec, omega, owners):
    mode_scale = 1.0 / jnp.sqrt(2.0 * omega)
    cos_phase = jnp.cos(q_angle)[:, None, None]
    sin_phase = jnp.sin(q_angle)[:, None, None]
    real_part = eigvec[0][None]
    imag_part = eigvec[1][None]
    coef_re = ((cos_phase * real_part - sin_phase * imag_part) * mode_scale).astype(jnp.bfloat16)
    coef_im = ((sin_phase * real_part + cos_phase * imag_part) * mode_scale).astype(jnp.bfloat16)
    table = jnp.stack([jnp.stack([coef_re, coef_im], 2), jnp.stack([-coef_im, coef_re], 2)], 2)
    cells, disp = table.shape[:2]
    return table.reshape(cells, disp, 2, 2, owners, -1).transpose(0, 1, 2, 4, 3, 5)


def kernel(
    nph, nka, part_ref, kpt_ref, cell_ref, out_ref,
    core_send, core_recv, x_send, x_recv, mine, vert_send, vert_recv, vert_f32, turned,
    k_mine, k_all, cos_re, cos_im, str_send, str_recv,
    core_ss, core_rs, x_ss, x_rs, v_ss, v_rs, k_ss, k_rs, s_ss, s_rs,
):
    ph, ka = lax.axis_index("ph"), lax.axis_index("ka")
    nx = nph // 2
    core, x = lax.rem(ph, 2), lax.div(ph, 2)
    mate = 2 * x + (1 - core)
    cells, rows_all, width = part_ref.shape
    rows = rows_all // nph
    wsplit, msplit = splits(nka, width)
    grouped = rows // msplit
    modes = grouped // 2
    wblk = width // wsplit
    block_rows = cells * grouped
    nloc = wblk // W
    kdev = kpt_ref.shape[1]
    all_cells = cell_ref.shape[0]

    barrier = pltpu.get_barrier_semaphore()
    pl.semaphore_signal(barrier, inc=1, device_id=(mate, ka), device_id_type=MESH)
    for step in range(1, nx):
        there = 2 * lax.rem(x + step, nx) + core
        pl.semaphore_signal(barrier, inc=1, device_id=(there, ka), device_id_type=MESH)
    for step in range(1, nka):
        there = lax.rem(ka + step, nka)
        pl.semaphore_signal(barrier, inc=1, device_id=(ph, there), device_id_type=MESH)

    for step in range(nx):
        owner = 2 * lax.rem(x + step, nx) + (1 - core)
        for cell in range(cells):
            block = part_ref[cell, pl.ds(pl.multiple_of(owner * rows, 8), rows), :]
            for group in range(msplit):
                at = group * block_rows + cell * grouped
                mine[at : at + grouped, :] = block[group * grouped : (group + 1) * grouped]
        core_send[step] = mine[...].astype(jnp.bfloat16)
    k_mine[...] = jnp.zeros_like(k_mine)
    k_mine[0:3, :] = kpt_ref[...]
    pl.semaphore_wait(barrier, nx + nka - 1)

    core_copies = []
    for step in range(nx - 1, -1, -1):
        copy = pltpu.make_async_remote_copy(
            src_ref=core_send.at[step], dst_ref=core_recv.at[step],
            send_sem=core_ss.at[step], recv_sem=core_rs.at[step],
            device_id=(mate, ka), device_id_type=MESH,
        )
        copy.start()
        core_copies.append((step, copy))
    k_copies = []
    for step in range(1, nka):
        there = lax.rem(ka + step, nka)
        copy = pltpu.make_async_remote_copy(
            src_ref=k_mine, dst_ref=k_all.at[ka],
            send_sem=k_ss.at[step], recv_sem=k_rs.at[ka],
            device_id=(ph, there), device_id_type=MESH,
        )
        copy.start()
        k_copies.append(copy)
    k_all[ka] = k_mine[...]

    x_copies = []
    for step, copy in core_copies:
        owner = 2 * lax.rem(x + step, nx) + core
        for cell in range(cells):
            block = part_ref[cell, pl.ds(pl.multiple_of(owner * rows, 8), rows), :]
            for group in range(msplit):
                at = group * block_rows + cell * grouped
                mine[at : at + grouped, :] = block[group * grouped : (group + 1) * grouped]
        copy.wait_recv()
        mine[...] += core_recv[step].astype(jnp.float32)
        if step > 0:
            x_send[step - 1] = mine[...].astype(jnp.bfloat16)
            send = pltpu.make_async_remote_copy(
                src_ref=x_send.at[step - 1], dst_ref=x_recv.at[step - 1],
                send_sem=x_ss.at[step - 1], recv_sem=x_rs.at[step - 1],
                device_id=(owner, ka), device_id_type=MESH,
            )
            send.start()
            x_copies.append((step, send))

    for step in range(nka):
        src = lax.rem(ka + step, nka)
        if step:
            pltpu.make_async_remote_copy(
                src_ref=k_mine, dst_ref=k_all.at[src],
                send_sem=k_ss.at[step], recv_sem=k_rs.at[src],
                device_id=(ph, src), device_id_type=MESH,
            ).wait_recv()
    def phases(src, carry):
        numer = k_all[src]
        summed = (
            cell_ref[:, 0:1] * numer[0:1, :]
            + cell_ref[:, 1:2] * numer[1:2, :]
            + cell_ref[:, 2:3] * numer[2:3, :]
        )
        angle = jnp.bitwise_and(summed, KGRID - 1).astype(jnp.float32) * (2.0 * math.pi / KGRID)
        cosine, sine = jnp.cos(angle), jnp.sin(angle)
        cos_re[src] = jnp.concatenate([cosine, -sine], 0).astype(jnp.bfloat16)
        cos_im[src] = jnp.concatenate([sine, cosine], 0).astype(jnp.bfloat16)
        return carry

    lax.fori_loop(0, nka, phases, 0)

    for step, send in x_copies:
        send.wait_recv()
        mine[...] += x_recv[step - 1].astype(jnp.float32)

    for step in range(nka):
        group, part = divmod(step, wsplit)
        vert_send[step] = mine[
            group * block_rows : (group + 1) * block_rows, part * wblk : (part + 1) * wblk
        ].astype(jnp.bfloat16)
    v_copies = []
    for step in range(1, nka):
        there = lax.rem(ka + step, nka)
        copy = pltpu.make_async_remote_copy(
            src_ref=vert_send.at[there], dst_ref=vert_recv.at[ka],
            send_sem=v_ss.at[step], recv_sem=v_rs.at[ka],
            device_id=(ph, there), device_id_type=MESH,
        )
        copy.start()
        v_copies.append(copy)
    vert_recv[ka] = vert_send[ka]
    for step in range(1, nka):
        src = lax.rem(ka + step, nka)
        pltpu.make_async_remote_copy(
            src_ref=vert_send.at[src], dst_ref=vert_recv.at[src],
            send_sem=v_ss.at[step], recv_sem=v_rs.at[src],
            device_id=(ph, src), device_id_type=MESH,
        ).wait_recv()
    for src in range(nka):
        vert_f32[src * block_rows : (src + 1) * block_rows, :] = vert_recv[src].astype(jnp.float32)
    for mode in range(modes):
        real = vert_f32[pl.ds(mode, all_cells, stride=grouped), :]
        imag = vert_f32[pl.ds(modes + mode, all_cells, stride=grouped), :]
        turned[mode] = jnp.concatenate([real, imag], 0).T.astype(jnp.bfloat16)

    def strengths(step, carry):
        there = lax.rem(ka + step + 1, nka)
        phase_re, phase_im = cos_re[there], cos_im[there]
        for mode in range(modes):
            left = turned[mode]
            bloch_re = jnp.dot(left, phase_re, preferred_element_type=jnp.float32)
            bloch_im = jnp.dot(left, phase_im, preferred_element_type=jnp.float32)
            squares = bloch_re * bloch_re + bloch_im * bloch_im
            str_send[there, mode * nloc : (mode + 1) * nloc, :] = jnp.sum(
                squares.reshape(nloc, W, kdev), axis=1
            )

        @pl.when(step < nka - 1)
        def _():
            pltpu.make_async_remote_copy(
                src_ref=str_send.at[there], dst_ref=str_recv.at[ka],
                send_sem=s_ss.at[there], recv_sem=s_rs.at[ka],
                device_id=(ph, there), device_id_type=MESH,
            ).start()

        return carry

    lax.fori_loop(0, nka, strengths, 0)
    str_recv[ka] = str_send[ka]
    for step in range(1, nka):
        src = lax.rem(ka + step, nka)
        pltpu.make_async_remote_copy(
            src_ref=str_send.at[src], dst_ref=str_recv.at[src],
            send_sem=s_ss.at[src], recv_sem=s_rs.at[src],
            device_id=(ph, src), device_id_type=MESH,
        ).wait()
    for src in range(nka):
        for mode in range(modes):
            group, part = divmod(src, wsplit)
            out_ref[group * modes + mode, part * nloc : (part + 1) * nloc, :] = str_recv[
                src, mode * nloc : (mode + 1) * nloc, :
            ]
    for step, copy in core_copies:
        copy.wait_send()
    for step, copy in x_copies:
        copy.wait_send()
    for copy in k_copies + v_copies:
        copy.wait_send()


def shards(g_wan, el_cells, ph_cells, q_point, kpoints, eigvec, omega):
    nph, nka = lax.axis_size("ph"), lax.axis_size("ka")
    q_angle = angles(q_point[:, None], ph_cells)[0]
    wsplit, msplit = splits(nka, g_wan.shape[-1])
    table = coupling(q_angle, eigvec, omega, nph * msplit)
    partial_terms = jnp.einsum(
        "pncqom,epncw->eqomw", table, g_wan, preferred_element_type=jnp.float32
    )
    cells, width = g_wan.shape[0], g_wan.shape[-1]
    mode_total = eigvec.shape[-1]
    modes = mode_total // nph
    partial_terms = partial_terms.reshape(cells, 2 * mode_total, width)
    kdev, all_cells = kpoints.shape[1], el_cells.shape[1]
    nx, wblk = nph // 2, width // wsplit
    nloc = wblk // W
    rows = cells * 2 * modes
    grouped = modes // msplit
    block_rows = cells * 2 * grouped
    bf16, f32 = jnp.bfloat16, jnp.float32
    vmem, dma = pltpu.VMEM, pltpu.SemaphoreType.DMA
    summed = pl.pallas_call(
        functools.partial(kernel, nph, nka),
        out_shape=jax.ShapeDtypeStruct((modes, W, kdev), f32),
        in_specs=[pl.BlockSpec(memory_space=vmem)] * 3,
        out_specs=pl.BlockSpec(memory_space=vmem),
        scratch_shapes=[
            vmem((nx, rows, width), bf16),
            vmem((nx, rows, width), bf16),
            vmem((nx - 1, rows, width), bf16),
            vmem((nx - 1, rows, width), bf16),
            vmem((rows, width), f32),
            vmem((nka, block_rows, wblk), bf16),
            vmem((nka, block_rows, wblk), bf16),
            vmem((nka * block_rows, wblk), f32),
            vmem((grouped, wblk, 2 * all_cells), bf16),
            vmem((8, kdev), jnp.int32),
            vmem((nka, 8, kdev), jnp.int32),
            vmem((nka, 2 * all_cells, kdev), bf16),
            vmem((nka, 2 * all_cells, kdev), bf16),
            vmem((nka, grouped * nloc, kdev), f32),
            vmem((nka, grouped * nloc, kdev), f32),
            dma((nx,)), dma((nx,)), dma((nx - 1,)), dma((nx - 1,)),
            dma((nka,)), dma((nka,)), dma((nka,)), dma((nka,)), dma((nka,)), dma((nka,)),
        ],
        compiler_params=pltpu.CompilerParams(
            collective_id=0, has_side_effects=True, vmem_limit_bytes=56 * 1024 * 1024
        ),
    )(partial_terms, kpoints, el_cells.T)
    normalizer = float(all_cells * g_wan.shape[1] * nph * W)
    return summed / normalizer


def solution(mesh):
    return jax.shard_map(
        shards,
        mesh=mesh,
        in_specs=(
            P("ka", "ph", None, None, None),
            P(),
            P(None, "ph"),
            P(),
            P(None, "ka"),
            P(),
            P(),
        ),
        out_specs=P("ph", None, "ka"),
        check_vma=False,
    )
```

```python
import functools
import math

import jax
import jax.numpy as jnp
from jax import lax
from jax.experimental import pallas as pl
from jax.experimental.pallas import tpu as pltpu
from jax.sharding import PartitionSpec as P

W = 32
KGRID = 64
LANES = 128
MESH = pl.DeviceIdType.MESH


def splits(ways, width):
    by_width = math.gcd(ways, width // W)
    return by_width, ways // by_width


def cell_groups(cells, grouped):
    return 2 if cells % 2 == 0 and (cells // 2 * grouped) % 16 == 0 else 1


def turn(numerator):
    folded = numerator - KGRID * jnp.floor(numerator * (1.0 / KGRID))
    return folded * (2.0 * math.pi / KGRID)


def kernel(
    nph, nka, normalizer, g_ref, kpt_ref, cell_ref, q_ref, phc_ref, eig_ref, omega_ref, out_ref,
    g_buf, table, part, core_send, core_recv, x_send, x_recv, vert_send, vert_recv, vert_f32, turned,
    k_mine, k_all, cos_re, cos_im, str_send, str_recv,
    g_sem, core_ss, core_rs, x_ss, x_rs, v_ss, v_rs, k_ss, k_rs, s_ss, s_rs,
):
    ph, ka = lax.axis_index("ph"), lax.axis_index("ka")
    nx = nph // 2
    core, x = lax.rem(ph, 2), lax.div(ph, 2)
    mate = 2 * x + (1 - core)
    cells, pairs, tiles = g_ref.shape[:3]
    depth = 2 * pairs
    width = tiles * LANES
    rows_all = part.shape[1]
    rows = rows_all // nph
    wsplit, msplit = splits(nka, width)
    grouped = rows // msplit
    modes = grouped // 2
    wblk = width // wsplit
    nloc = wblk // W
    block_rows = cells * grouped
    groups = cell_groups(cells, grouped)
    group_cells = cells // groups
    group_rows = group_cells * grouped
    halves = 2
    half = width // halves
    kdev = kpt_ref.shape[1]
    all_cells = cell_ref.shape[1]
    mode_total = omega_ref.shape[1]
    disp = eig_ref.shape[1]

    chunks = [(g, h) for g in range(groups) for h in range(halves)]
    tiles_half = tiles // halves
    g_copies = {}
    for g, h in chunks:
        for cell in range(g * group_cells, (g + 1) * group_cells):
            for tile in range(h * tiles_half, (h + 1) * tiles_half):
                copy = pltpu.make_async_copy(
                    g_ref.at[cell, :, tile], g_buf.at[cell, tile], g_sem.at[cell, tile]
                )
                copy.start()
                g_copies[cell, tile] = copy

    barrier = pltpu.get_barrier_semaphore()
    pl.semaphore_signal(barrier, inc=1, device_id=(mate, ka), device_id_type=MESH)
    for step in range(1, nx):
        there = 2 * lax.rem(x + step, nx) + core
        pl.semaphore_signal(barrier, inc=1, device_id=(there, ka), device_id_type=MESH)
    for step in range(1, nka):
        there = lax.rem(ka + step, nka)
        pl.semaphore_signal(barrier, inc=1, device_id=(ph, there), device_id_type=MESH)

    spread_v = lax.broadcasted_iota(jnp.int32, (disp, 2 * disp), 0)
    spread_col = lax.broadcasted_iota(jnp.int32, (disp, 2 * disp), 1)
    even = (spread_col == 2 * spread_v).astype(jnp.float32)
    odd = (spread_col == 2 * spread_v + 1).astype(jnp.float32)

    def spread(values, pattern):
        return lax.dot_general(
            values, pattern, (((0,), (0,)), ((), ())),
            preferred_element_type=jnp.float32, precision=lax.Precision.HIGHEST,
        )

    real, imag = eig_ref[0], eig_ref[1]
    first = spread(real, even) - spread(imag, odd)
    second = spread(imag, even) + spread(real, odd)

    def by_owner(upper, lower):
        pieces = []
        for at in range(0, mode_total, modes):
            pieces += [upper[at : at + modes], lower[at : at + modes]]
        return jnp.concatenate(pieces, 0)

    scale = 1.0 / jnp.sqrt(2.0 * jnp.broadcast_to(omega_ref[...], (2 * disp, mode_total)).T)
    scale = by_owner(scale, scale)
    with_cos = by_owner(first, second)
    with_sin = by_owner(-second, first)
    numer = (
        q_ref[0] * phc_ref[0:1, :] + q_ref[1] * phc_ref[1:2, :] + q_ref[2] * phc_ref[2:3, :]
    )
    q_angle = jnp.bitwise_and(numer, KGRID - 1).astype(jnp.float32) * (2.0 * math.pi / KGRID)
    q_cos, q_sin = jnp.cos(q_angle), jnp.sin(q_angle)
    pieces = []
    for p in range(phc_ref.shape[1]):
        pieces.append(
            (with_cos * q_cos[:, p : p + 1] + with_sin * q_sin[:, p : p + 1]) * scale
        )
    table[...] = jnp.concatenate(pieces, 1).astype(jnp.bfloat16)

    k_mine[...] = jnp.zeros_like(k_mine)
    k_mine[0:3, :] = kpt_ref[...].astype(jnp.float32)
    pl.semaphore_wait(barrier, nx + nka - 1)
    k_copies = []
    for step in range(1, nka):
        there = lax.rem(ka + step, nka)
        copy = pltpu.make_async_remote_copy(
            src_ref=k_mine, dst_ref=k_all.at[ka],
            send_sem=k_ss.at[step], recv_sem=k_rs.at[ka],
            device_id=(ph, there), device_id_type=MESH,
        )
        copy.start()
        k_copies.append(copy)
    k_all[ka] = k_mine[...]

    def owned(owner, index):
        g, h = chunks[index]
        blocks = [
            part[cell, pl.ds(pl.multiple_of(owner * rows, 8), rows), h * half : (h + 1) * half]
            for cell in range(g * group_cells, (g + 1) * group_cells)
        ]
        return jnp.concatenate(
            [
                block[group * grouped : (group + 1) * grouped]
                for group in range(msplit)
                for block in blocks
            ],
            0,
        )

    def multiply(index):
        g, h = chunks[index]
        for cell in range(g * group_cells, (g + 1) * group_cells):
            for tile in range(h * tiles_half, (h + 1) * tiles_half, 2):
                g_copies[cell, tile].wait()
                g_copies[cell, tile + 1].wait()
                right = jnp.concatenate(
                    [
                        g_buf[cell, tile].reshape(depth, LANES),
                        g_buf[cell, tile + 1].reshape(depth, LANES),
                    ],
                    1,
                )
                part[cell, :, tile * LANES : (tile + 2) * LANES] = jnp.dot(
                    table[...], right, preferred_element_type=jnp.float32
                )

    core_copies, x_copies, v_copies = {}, {}, []

    def to_mate(index):
        for step in range(nx - 1, -1, -1):
            owner = 2 * lax.rem(x + step, nx) + (1 - core)
            core_send[index, step] = owned(owner, index).astype(jnp.bfloat16)
            copy = pltpu.make_async_remote_copy(
                src_ref=core_send.at[index, step], dst_ref=core_recv.at[index, step],
                send_sem=core_ss.at[index, step], recv_sem=core_rs.at[index, step],
                device_id=(mate, ka), device_id_type=MESH,
            )
            copy.start()
            core_copies[index, step] = copy

    def to_other_chips(index):
        for step in range(1, nx):
            owner = 2 * lax.rem(x + step, nx) + core
            core_copies[index, step].wait_recv()
            both = owned(owner, index) + core_recv[index, step].astype(jnp.float32)
            x_send[index, step - 1] = both.astype(jnp.bfloat16)
            copy = pltpu.make_async_remote_copy(
                src_ref=x_send.at[index, step - 1], dst_ref=x_recv.at[index, step - 1],
                send_sem=x_ss.at[index, step - 1], recv_sem=x_rs.at[index, step - 1],
                device_id=(owner, ka), device_id_type=MESH,
            )
            copy.start()
            x_copies[index, step] = copy

    def vertices(index):
        g, h = chunks[index]
        core_copies[index, 0].wait_recv()
        total = owned(ph, index) + core_recv[index, 0].astype(jnp.float32)
        for step in range(1, nx):
            x_copies[index, step].wait_recv()
            total = total + x_recv[index, step - 1].astype(jnp.float32)
        total = total.astype(jnp.bfloat16)
        here = wsplit // halves
        for group in range(msplit):
            for local in range(here):
                vert_send[group * wsplit + h * here + local, g] = total[
                    group * group_rows : (group + 1) * group_rows,
                    local * wblk : (local + 1) * wblk,
                ]
        for group in range(msplit):
            for local in range(here):
                there = group * wsplit + h * here + lax.rem(local + ka, here)

                @pl.when(there != ka)
                def _():
                    pltpu.make_async_remote_copy(
                        src_ref=vert_send.at[there, g], dst_ref=vert_recv.at[ka, g],
                        send_sem=v_ss.at[there, g], recv_sem=v_rs.at[ka, g],
                        device_id=(ph, there), device_id_type=MESH,
                    ).start()

                @pl.when(there == ka)
                def _():
                    vert_recv[ka, g] = vert_send[there, g]

    count = len(chunks)
    for index in range(count):
        multiply(index)
        to_mate(index)
        if index >= 1:
            to_other_chips(index - 1)
        if index >= 3:
            vertices(index - 3)
    to_other_chips(count - 1)
    for index in range(max(count - 3, 0), count - 1):
        vertices(index)

    for step in range(1, nka):
        src = lax.rem(ka + step, nka)
        pltpu.make_async_remote_copy(
            src_ref=k_mine, dst_ref=k_all.at[src],
            send_sem=k_ss.at[step], recv_sem=k_rs.at[src],
            device_id=(ph, src), device_id_type=MESH,
        ).wait_recv()
    el_cells = jnp.concatenate(
        [cell_ref[...].astype(jnp.float32), jnp.zeros((5, all_cells), jnp.float32)], 0
    )

    def phases(src, carry):
        angle = turn(
            lax.dot_general(
                el_cells, k_all[src], (((0,), (0,)), ((), ())), preferred_element_type=jnp.float32
            )
        )
        cosine, sine = jnp.cos(angle), jnp.sin(angle)
        cos_re[src] = jnp.concatenate([cosine, -sine], 0).astype(jnp.bfloat16)
        cos_im[src] = jnp.concatenate([sine, cosine], 0).astype(jnp.bfloat16)
        return carry

    lax.fori_loop(0, nka, phases, 0)
    vertices(count - 1)

    for step in range(1, nka):
        src = lax.rem(ka + step, nka)
        for g in range(groups):
            pltpu.make_async_remote_copy(
                src_ref=vert_send.at[src, g], dst_ref=vert_recv.at[src, g],
                send_sem=v_ss.at[src, g], recv_sem=v_rs.at[src, g],
                device_id=(ph, src), device_id_type=MESH,
            ).wait()
    for src in range(nka):
        for g in range(groups):
            at = src * block_rows + g * group_rows
            vert_f32[at : at + group_rows, :] = vert_recv[src, g].astype(jnp.float32)
    for mode in range(modes):
        re_rows = vert_f32[pl.ds(mode, all_cells, stride=grouped), :]
        im_rows = vert_f32[pl.ds(modes + mode, all_cells, stride=grouped), :]
        turned[mode * wblk : (mode + 1) * wblk, :] = (
            jnp.concatenate([re_rows, im_rows], 0).T.astype(jnp.bfloat16)
        )

    batch = 4 if modes % 4 == 0 else 1

    def strengths(step, carry):
        there = lax.rem(ka + step + 1, nka)
        phase_re, phase_im = cos_re[there], cos_im[there]
        for mode in range(0, modes, batch):
            left = turned[mode * wblk : (mode + batch) * wblk, :]
            bloch_re = jnp.dot(left, phase_re, preferred_element_type=jnp.float32)
            bloch_im = jnp.dot(left, phase_im, preferred_element_type=jnp.float32)
            squares = bloch_re * bloch_re + bloch_im * bloch_im
            str_send[there, mode * nloc : (mode + batch) * nloc, :] = (
                jnp.sum(squares.reshape(batch * nloc, W, kdev), axis=1) / normalizer
            )

        @pl.when(step < nka - 1)
        def _():
            pltpu.make_async_remote_copy(
                src_ref=str_send.at[there], dst_ref=str_recv.at[ka],
                send_sem=s_ss.at[there], recv_sem=s_rs.at[ka],
                device_id=(ph, there), device_id_type=MESH,
            ).start()

        return carry

    lax.fori_loop(0, nka, strengths, 0)

    def place(src, held):
        group, piece = divmod(src, wsplit)
        for mode in range(modes):
            out_ref[group * modes + mode, piece * nloc : (piece + 1) * nloc, :] = held[
                src, mode * nloc : (mode + 1) * nloc, :
            ]

    str_recv[ka] = str_send[ka]
    for step in range(1, nka):
        src = lax.rem(ka + step, nka)
        pltpu.make_async_remote_copy(
            src_ref=str_send.at[src], dst_ref=str_recv.at[src],
            send_sem=s_ss.at[src], recv_sem=s_rs.at[src],
            device_id=(ph, src), device_id_type=MESH,
        ).wait()
    for src in range(nka):
        place(src, str_recv)
    for copy in list(core_copies.values()) + list(x_copies.values()) + k_copies:
        copy.wait_send()


def shards(g_wan, el_cells, ph_cells, q_point, kpoints, eigvec, omega):
    nph, nka = lax.axis_size("ph"), lax.axis_size("ka")
    cells, ph_loc, disp, parts, width = g_wan.shape
    tiles = width // LANES
    g_view = g_wan.reshape(cells, ph_loc * disp, parts, tiles, LANES).transpose(0, 1, 3, 2, 4)
    wsplit, msplit = splits(nka, width)
    mode_total = eigvec.shape[-1]
    modes = mode_total // nph
    kdev, all_cells = kpoints.shape[1], el_cells.shape[1]
    nx, wblk = nph // 2, width // wsplit
    nloc = wblk // W
    mode_group = modes // msplit
    block_rows = cells * 2 * mode_group
    groups = cell_groups(cells, 2 * mode_group)
    group_rows = block_rows // groups
    chunks = groups * 2
    sent = (chunks, nx, msplit * group_rows, width // 2)
    passed = (chunks, nx - 1, msplit * group_rows, width // 2)
    bf16, f32 = jnp.bfloat16, jnp.float32
    vmem, dma = pltpu.VMEM, pltpu.SemaphoreType.DMA
    in_vmem, in_smem = pl.BlockSpec(memory_space=vmem), pl.BlockSpec(memory_space=pltpu.SMEM)
    normalizer = float(all_cells * ph_loc * nph * W)
    return pl.pallas_call(
        functools.partial(kernel, nph, nka, normalizer),
        out_shape=jax.ShapeDtypeStruct((modes, W, kdev), f32),
        in_specs=[
            pl.BlockSpec(memory_space=pl.ANY), in_vmem, in_vmem, in_smem, in_vmem, in_vmem, in_vmem
        ],
        out_specs=in_vmem,
        scratch_shapes=[
            vmem((cells, tiles, ph_loc * disp, parts, LANES), bf16),
            vmem((2 * mode_total, ph_loc * disp * parts), bf16),
            vmem((cells, 2 * mode_total, width), f32),
            vmem(sent, bf16),
            vmem(sent, bf16),
            vmem(passed, bf16),
            vmem(passed, bf16),
            vmem((nka, groups, group_rows, wblk), bf16),
            vmem((nka, groups, group_rows, wblk), bf16),
            vmem((nka * block_rows, wblk), f32),
            vmem((mode_group * wblk, 2 * all_cells), bf16),
            vmem((8, kdev), f32),
            vmem((nka, 8, kdev), f32),
            vmem((nka, 2 * all_cells, kdev), bf16),
            vmem((nka, 2 * all_cells, kdev), bf16),
            vmem((nka, mode_group * nloc, kdev), f32),
            vmem((nka, mode_group * nloc, kdev), f32),
            dma((cells, tiles)),
            dma(sent[:2]), dma(sent[:2]), dma(passed[:2]), dma(passed[:2]),
            dma((nka, groups)), dma((nka, groups)),
            dma((nka,)), dma((nka,)), dma((nka,)), dma((nka,)),
        ],
        compiler_params=pltpu.CompilerParams(
            collective_id=0, has_side_effects=True, vmem_limit_bytes=56 * 1024 * 1024
        ),
    )(g_view, kpoints, el_cells, q_point, ph_cells, eigvec, omega.reshape(1, mode_total))


def solution(mesh):
    return jax.shard_map(
        shards,
        mesh=mesh,
        in_specs=(
            P("ka", "ph", None, None, None),
            P(),
            P(None, "ph"),
            P(),
            P(None, "ka"),
            P(),
            P(),
        ),
        out_specs=P("ph", None, "ka"),
        check_vma=False,
    )
```

```python
import functools
import math

import jax
import jax.numpy as jnp
from jax import lax
from jax.experimental import pallas as pl
from jax.experimental.pallas import tpu as pltpu
from jax.sharding import PartitionSpec as P

W = 32
KGRID = 64
LANES = 128
MESH = pl.DeviceIdType.MESH


def team_size(nka):
    return nka // 2 if nka % 2 == 0 else nka


def splits(ways, width):
    by_width = math.gcd(ways, width // W)
    return by_width, ways // by_width


def cell_groups(cells, grouped):
    return 2 if cells % 2 == 0 and (cells // 2 * grouped) % 16 == 0 else 1


def cos_sin(numerator):
    folded = numerator - KGRID * jnp.floor(numerator * (1.0 / KGRID))
    quarter = jnp.floor((folded + KGRID // 8) * (4.0 / KGRID))
    angle = (folded - quarter * (KGRID // 4)) * (2.0 * math.pi / KGRID)
    square = angle * angle
    cosine = 1.0 + square * (
        -1 / 2 + square * (1 / 24 + square * (-1 / 720 + square * (1 / 40320)))
    )
    sine = angle + angle * square * (
        -1 / 6 + square * (1 / 120 + square * (-1 / 5040 + square * (1 / 362880)))
    )
    odd = (quarter == 1.0) | (quarter == 3.0)
    cos_minus = (quarter == 1.0) | (quarter == 2.0)
    sin_minus = (quarter == 2.0) | (quarter == 3.0)
    cos_all = jnp.where(odd, sine, cosine)
    sin_all = jnp.where(odd, cosine, sine)
    return jnp.where(cos_minus, -cos_all, cos_all), jnp.where(sin_minus, -sin_all, sin_all)


def kernel(
    nph, nka, normalizer, g_ref, kpt_ref, cell_ref, q_ref, phc_ref, eig_ref, omega_ref, out_ref,
    g_buf, table, part, core_send, core_recv, x_send, x_recv, vert_send, vert_recv, vert_f32, turned,
    k_mine, k_all, cos_re, cos_im, str_send, str_recv,
    g_sem, core_ss, core_rs, x_ss, x_rs, v_ss, v_rs, k_ss, k_rs, s_ss, s_rs,
):
    ph, ka = lax.axis_index("ph"), lax.axis_index("ka")
    nx = nph // 2
    core, x = lax.rem(ph, 2), lax.div(ph, 2)
    mate = 2 * x + (1 - core)
    cells, pairs, tiles = g_ref.shape[:3]
    depth = 2 * pairs
    width = tiles * LANES
    rows_all = part.shape[1]
    rows = rows_all // nph
    ways = team_size(nka)
    team, spot = lax.div(ka, ways), lax.rem(ka, ways)
    wsplit, msplit = splits(ways, width)
    grouped = rows // msplit
    modes = grouped // 2
    wblk = width // wsplit
    nloc = wblk // W
    lanes = vert_f32.shape[2]
    block_rows = cells * grouped
    groups = cell_groups(cells, grouped)
    group_cells = cells // groups
    group_rows = group_cells * grouped
    halves = 2
    half = width // halves
    kdev = kpt_ref.shape[1]
    all_cells = cell_ref.shape[1]
    mode_total = omega_ref.shape[1]
    disp = eig_ref.shape[1]

    chunks = [(g, h) for g in range(groups) for h in range(halves)]
    tiles_half = tiles // halves
    g_copies = {}
    for g, h in chunks:
        for cell in range(g * group_cells, (g + 1) * group_cells):
            for tile in range(h * tiles_half, (h + 1) * tiles_half):
                copy = pltpu.make_async_copy(
                    g_ref.at[cell, :, tile], g_buf.at[cell, tile], g_sem.at[cell, tile]
                )
                copy.start()
                g_copies[cell, tile] = copy

    barrier = pltpu.get_barrier_semaphore()
    pl.semaphore_signal(barrier, inc=1, device_id=(mate, ka), device_id_type=MESH)
    for step in range(1, nx):
        there = 2 * lax.rem(x + step, nx) + core
        pl.semaphore_signal(barrier, inc=1, device_id=(there, ka), device_id_type=MESH)
    for step in range(1, nka):
        there = lax.rem(ka + step, nka)
        pl.semaphore_signal(barrier, inc=1, device_id=(ph, there), device_id_type=MESH)

    spread_v = lax.broadcasted_iota(jnp.int32, (disp, 2 * disp), 0)
    spread_col = lax.broadcasted_iota(jnp.int32, (disp, 2 * disp), 1)
    even = (spread_col == 2 * spread_v).astype(jnp.float32)
    odd = (spread_col == 2 * spread_v + 1).astype(jnp.float32)

    def spread(values, pattern):
        return lax.dot_general(
            values, pattern, (((0,), (0,)), ((), ())),
            preferred_element_type=jnp.float32, precision=lax.Precision.HIGHEST,
        )

    real, imag = eig_ref[0], eig_ref[1]
    first = spread(real, even) - spread(imag, odd)
    second = spread(imag, even) + spread(real, odd)

    def by_owner(upper, lower):
        pieces = []
        for at in range(0, mode_total, modes):
            pieces += [upper[at : at + modes], lower[at : at + modes]]
        return jnp.concatenate(pieces, 0)

    scale = 1.0 / jnp.sqrt(2.0 * jnp.broadcast_to(omega_ref[...], (2 * disp, mode_total)).T)
    scale = by_owner(scale, scale)
    with_cos = by_owner(first, second)
    with_sin = by_owner(-second, first)
    numer = (
        q_ref[0] * phc_ref[0:1, :] + q_ref[1] * phc_ref[1:2, :] + q_ref[2] * phc_ref[2:3, :]
    )
    q_cos, q_sin = cos_sin(numer.astype(jnp.float32))
    pieces = []
    for p in range(phc_ref.shape[1]):
        pieces.append(
            (with_cos * q_cos[:, p : p + 1] + with_sin * q_sin[:, p : p + 1]) * scale
        )
    table[...] = jnp.concatenate(pieces, 1).astype(jnp.bfloat16)

    k_mine[...] = jnp.zeros_like(k_mine)
    k_mine[0:3, :] = kpt_ref[...].astype(jnp.float32)
    pl.semaphore_wait(barrier, nx + nka - 1)
    k_copies = []
    for step in range(1, ways):
        there = team * ways + lax.rem(spot + step, ways)
        copy = pltpu.make_async_remote_copy(
            src_ref=k_mine, dst_ref=k_all.at[spot],
            send_sem=k_ss.at[step], recv_sem=k_rs.at[spot],
            device_id=(ph, there), device_id_type=MESH,
        )
        copy.start()
        k_copies.append(copy)
    k_all[spot] = k_mine[...]

    def owned(owner, index):
        g, h = chunks[index]
        blocks = [
            part[cell, pl.ds(pl.multiple_of(owner * rows, 8), rows), h * half : (h + 1) * half]
            for cell in range(g * group_cells, (g + 1) * group_cells)
        ]
        return jnp.concatenate(
            [
                block[group * grouped : (group + 1) * grouped]
                for group in range(msplit)
                for block in blocks
            ],
            0,
        )

    def multiply(index):
        g, h = chunks[index]
        for cell in range(g * group_cells, (g + 1) * group_cells):
            for tile in range(h * tiles_half, (h + 1) * tiles_half, 2):
                g_copies[cell, tile].wait()
                g_copies[cell, tile + 1].wait()
                right = jnp.concatenate(
                    [
                        g_buf.at[cell, tile].reshape(depth, LANES)[...],
                        g_buf.at[cell, tile + 1].reshape(depth, LANES)[...],
                    ],
                    1,
                )
                part[cell, :, tile * LANES : (tile + 2) * LANES] = jnp.dot(
                    table[...], right, preferred_element_type=jnp.float32
                )

    core_copies, x_copies, v_copies = {}, {}, []

    def to_mate(index):
        for step in range(nx - 1, -1, -1):
            owner = 2 * lax.rem(x + step, nx) + (1 - core)
            core_send[index, step] = owned(owner, index).astype(jnp.bfloat16)
            copy = pltpu.make_async_remote_copy(
                src_ref=core_send.at[index, step], dst_ref=core_recv.at[index, step],
                send_sem=core_ss.at[index, step], recv_sem=core_rs.at[index, step],
                device_id=(mate, ka), device_id_type=MESH,
            )
            copy.start()
            core_copies[index, step] = copy

    def to_other_chips(index):
        for step in range(1, nx):
            owner = 2 * lax.rem(x + step, nx) + core
            core_copies[index, step].wait_recv()
            both = owned(owner, index) + core_recv[index, step].astype(jnp.float32)
            x_send[index, step - 1] = both.astype(jnp.bfloat16)
            copy = pltpu.make_async_remote_copy(
                src_ref=x_send.at[index, step - 1], dst_ref=x_recv.at[index, step - 1],
                send_sem=x_ss.at[index, step - 1], recv_sem=x_rs.at[index, step - 1],
                device_id=(owner, ka), device_id_type=MESH,
            )
            copy.start()
            x_copies[index, step] = copy

    def vertices(index):
        g, h = chunks[index]
        core_copies[index, 0].wait_recv()
        total = owned(ph, index) + core_recv[index, 0].astype(jnp.float32)
        for step in range(1, nx):
            x_copies[index, step].wait_recv()
            total = total + x_recv[index, step - 1].astype(jnp.float32)
        total = total.astype(jnp.bfloat16)
        here = wsplit // halves
        for group in range(msplit):
            for local in range(here):
                vert_send[group * wsplit + h * here + local, g] = total[
                    group * group_rows : (group + 1) * group_rows,
                    local * wblk : (local + 1) * wblk,
                ]
        for group in range(msplit):
            for local in range(here):
                block = group * wsplit + h * here + lax.rem(local + spot, here)
                for step in range(nka // ways - 1, -1, -1):
                    there = lax.rem(team + step, nka // ways) * ways + block

                    @pl.when(there != ka)
                    def _():
                        pltpu.make_async_remote_copy(
                            src_ref=vert_send.at[block, g], dst_ref=vert_recv.at[ka, g],
                            send_sem=v_ss.at[there, g], recv_sem=v_rs.at[ka, g],
                            device_id=(ph, there), device_id_type=MESH,
                        ).start()

                    @pl.when(there == ka)
                    def _():
                        vert_recv[ka, g] = vert_send[block, g]

    count = len(chunks)
    for index in range(count):
        multiply(index)
        to_mate(index)
        if index >= 1:
            to_other_chips(index - 1)
        if index >= 3:
            vertices(index - 3)
    to_other_chips(count - 1)
    for index in range(max(count - 3, 0), count - 1):
        vertices(index)

    for step in range(1, ways):
        src = lax.rem(spot + step, ways)
        pltpu.make_async_remote_copy(
            src_ref=k_mine, dst_ref=k_all.at[src],
            send_sem=k_ss.at[step], recv_sem=k_rs.at[src],
            device_id=(ph, team * ways + src), device_id_type=MESH,
        ).wait_recv()
    el_cells = jnp.concatenate(
        [cell_ref[...].astype(jnp.float32), jnp.zeros((5, all_cells), jnp.float32)], 0
    )

    def phases(src, carry):
        cosine, sine = cos_sin(
            lax.dot_general(
                el_cells, k_all[src], (((0,), (0,)), ((), ())), preferred_element_type=jnp.float32
            )
        )
        cos_re[src] = jnp.concatenate([cosine, -sine], 0).astype(jnp.bfloat16)
        cos_im[src] = jnp.concatenate([sine, cosine], 0).astype(jnp.bfloat16)
        return carry

    lax.fori_loop(0, ways, phases, 0)
    vertices(count - 1)

    for step in range(1, nka):
        src = lax.rem(ka + step, nka)
        for g in range(groups):
            pltpu.make_async_remote_copy(
                src_ref=vert_send.at[lax.rem(src, ways), g], dst_ref=vert_recv.at[src, g],
                send_sem=v_ss.at[src, g], recv_sem=v_rs.at[src, g],
                device_id=(ph, src), device_id_type=MESH,
            ).wait()
    for src in range(nka):
        for g in range(groups):
            at = src * block_rows + g * group_rows
            block = vert_recv[src, g].astype(jnp.float32)
            for tile in range(vert_f32.shape[0]):
                vert_f32[tile, at : at + group_rows, :] = block[:, tile * lanes : (tile + 1) * lanes]
    for mode in range(modes):
        for tile in range(vert_f32.shape[0]):
            re_rows = vert_f32[tile, pl.ds(mode, all_cells, stride=grouped), :]
            im_rows = vert_f32[tile, pl.ds(modes + mode, all_cells, stride=grouped), :]
            at = mode * wblk + tile * lanes
            turned[at : at + lanes, :] = (
                jnp.concatenate([re_rows, im_rows], 0).T.astype(jnp.bfloat16)
            )

    batch = 2 if modes % 2 == 0 else 1

    def strengths(step, carry):
        there = lax.rem(spot + step + 1, ways)
        phase_re, phase_im = cos_re[there], cos_im[there]
        for mode in range(0, modes, batch):
            left = turned[mode * wblk : (mode + batch) * wblk, :]
            bloch_re = jnp.dot(left, phase_re, preferred_element_type=jnp.float32)
            bloch_im = jnp.dot(left, phase_im, preferred_element_type=jnp.float32)
            squares = bloch_re * bloch_re + bloch_im * bloch_im
            str_send[there, mode * nloc : (mode + batch) * nloc, :] = (
                jnp.sum(squares.reshape(batch * nloc, W, kdev), axis=1) / normalizer
            )

        @pl.when(step < ways - 1)
        def _():
            pltpu.make_async_remote_copy(
                src_ref=str_send.at[there], dst_ref=str_recv.at[spot],
                send_sem=s_ss.at[there], recv_sem=s_rs.at[spot],
                device_id=(ph, team * ways + there), device_id_type=MESH,
            ).start()

        return carry

    lax.fori_loop(0, ways, strengths, 0)

    def place(src, held):
        group, piece = divmod(src, wsplit)
        for mode in range(modes):
            out_ref[group * modes + mode, piece * nloc : (piece + 1) * nloc, :] = held[
                src, mode * nloc : (mode + 1) * nloc, :
            ]

    str_recv[spot] = str_send[spot]
    for step in range(1, ways):
        src = lax.rem(spot + step, ways)
        pltpu.make_async_remote_copy(
            src_ref=str_send.at[src], dst_ref=str_recv.at[src],
            send_sem=s_ss.at[src], recv_sem=s_rs.at[src],
            device_id=(ph, team * ways + src), device_id_type=MESH,
        ).wait()
    for src in range(ways):
        place(src, str_recv)
    for copy in list(core_copies.values()) + list(x_copies.values()) + k_copies:
        copy.wait_send()


def shards(g_wan, el_cells, ph_cells, q_point, kpoints, eigvec, omega):
    nph, nka = lax.axis_size("ph"), lax.axis_size("ka")
    cells, ph_loc, disp, parts, width = g_wan.shape
    tiles = width // LANES
    g_view = g_wan.reshape(cells, ph_loc * disp, parts, tiles, LANES).transpose(0, 1, 3, 2, 4)
    ways = team_size(nka)
    wsplit, msplit = splits(ways, width)
    mode_total = eigvec.shape[-1]
    modes = mode_total // nph
    kdev, all_cells = kpoints.shape[1], el_cells.shape[1]
    nx, wblk = nph // 2, width // wsplit
    nloc = wblk // W
    lanes = math.gcd(wblk, LANES)
    mode_group = modes // msplit
    block_rows = cells * 2 * mode_group
    groups = cell_groups(cells, 2 * mode_group)
    group_rows = block_rows // groups
    chunks = groups * 2
    sent = (chunks, nx, msplit * group_rows, width // 2)
    passed = (chunks, nx - 1, msplit * group_rows, width // 2)
    bf16, f32 = jnp.bfloat16, jnp.float32
    vmem, dma = pltpu.VMEM, pltpu.SemaphoreType.DMA
    in_vmem, in_smem = pl.BlockSpec(memory_space=vmem), pl.BlockSpec(memory_space=pltpu.SMEM)
    normalizer = float(all_cells * ph_loc * nph * W)
    return pl.pallas_call(
        functools.partial(kernel, nph, nka, normalizer),
        out_shape=jax.ShapeDtypeStruct((modes, W, kdev), f32),
        in_specs=[
            pl.BlockSpec(memory_space=pl.ANY), in_vmem, in_vmem, in_smem, in_vmem, in_vmem, in_vmem
        ],
        out_specs=in_vmem,
        scratch_shapes=[
            vmem((cells, tiles, ph_loc * disp, parts, LANES), bf16),
            vmem((2 * mode_total, ph_loc * disp * parts), bf16),
            vmem((cells, 2 * mode_total, width), f32),
            vmem(sent, bf16),
            vmem(sent, bf16),
            vmem(passed, bf16),
            vmem(passed, bf16),
            vmem((ways, groups, group_rows, wblk), bf16),
            vmem((nka, groups, group_rows, wblk), bf16),
            vmem((wblk // lanes, nka * block_rows, lanes), f32),
            vmem((mode_group * wblk, 2 * all_cells), bf16),
            vmem((8, kdev), f32),
            vmem((ways, 8, kdev), f32),
            vmem((ways, 2 * all_cells, kdev), bf16),
            vmem((ways, 2 * all_cells, kdev), bf16),
            vmem((ways, mode_group * nloc, kdev), f32),
            vmem((ways, mode_group * nloc, kdev), f32),
            dma((cells, tiles)),
            dma(sent[:2]), dma(sent[:2]), dma(passed[:2]), dma(passed[:2]),
            dma((nka, groups)), dma((nka, groups)),
            dma((ways,)), dma((ways,)), dma((ways,)), dma((ways,)),
        ],
        compiler_params=pltpu.CompilerParams(
            collective_id=0, has_side_effects=True, vmem_limit_bytes=52 * 1024 * 1024
        ),
    )(g_view, kpoints, el_cells, q_point, ph_cells, eigvec, omega.reshape(1, mode_total))


def solution(mesh):
    return jax.shard_map(
        shards,
        mesh=mesh,
        in_specs=(
            P("ka", "ph", None, None, None),
            P(),
            P(None, "ph"),
            P(),
            P(None, "ka"),
            P(),
            P(),
        ),
        out_specs=P("ph", None, "ka"),
        check_vma=False,
    )
```

```python
import functools
import math

import jax
import jax.numpy as jnp
from jax import lax
from jax.experimental import pallas as pl
from jax.experimental.pallas import tpu as pltpu
from jax.sharding import PartitionSpec as P

W = 32
KGRID = 64
LANES = 128
MESH = pl.DeviceIdType.MESH


def team_size(nka):
    return nka // 2 if nka % 2 == 0 else nka


def splits(ways, width):
    by_width = math.gcd(ways, width // W)
    return by_width, ways // by_width


def cell_groups(cells, grouped):
    return 2 if cells % 2 == 0 and (cells // 2 * grouped) % 16 == 0 else 1


def lands_in_place(nloc, msplit):
    return nloc % 8 == 0 and msplit == 1


def cos_sin(numerator):
    folded = numerator - KGRID * jnp.floor(numerator * (1.0 / KGRID))
    quarter = jnp.floor((folded + KGRID // 8) * (4.0 / KGRID))
    angle = (folded - quarter * (KGRID // 4)) * (2.0 * math.pi / KGRID)
    square = angle * angle
    cosine = 1.0 + square * (
        -1 / 2 + square * (1 / 24 + square * (-1 / 720 + square * (1 / 40320)))
    )
    sine = angle + angle * square * (
        -1 / 6 + square * (1 / 120 + square * (-1 / 5040 + square * (1 / 362880)))
    )
    odd = (quarter == 1.0) | (quarter == 3.0)
    cos_minus = (quarter == 1.0) | (quarter == 2.0)
    sin_minus = (quarter == 2.0) | (quarter == 3.0)
    cos_all = jnp.where(odd, sine, cosine)
    sin_all = jnp.where(odd, cosine, sine)
    return jnp.where(cos_minus, -cos_all, cos_all), jnp.where(sin_minus, -sin_all, sin_all)


def kernel(
    nph, nka, normalizer, g_ref, kpt_hbm, cell_hbm, q_hbm, phc_hbm, eig_hbm, omega_hbm, out_ref,
    kpt_ref, cell_ref, q_ref, phc_ref, eig_ref, omega_ref, small_sem,
    g_buf, table, part, core_send, core_recv, x_send, x_recv, vert_send, vert_recv, vert_f32, turned,
    k_mine, k_all, cos_re, cos_im, str_send, str_recv,
    g_sem, core_ss, core_rs, x_ss, x_rs, v_ss, v_rs, k_ss, k_rs, s_ss, s_rs,
):
    ph, ka = lax.axis_index("ph"), lax.axis_index("ka")
    nx = nph // 2
    core, x = lax.rem(ph, 2), lax.div(ph, 2)
    mate = 2 * x + (1 - core)
    cells, pairs, tiles = g_ref.shape[:3]
    depth = 2 * pairs
    width = tiles * LANES
    rows_all = part.shape[1]
    rows = rows_all // nph
    ways = team_size(nka)
    team, spot = lax.div(ka, ways), lax.rem(ka, ways)
    wsplit, msplit = splits(ways, width)
    grouped = rows // msplit
    modes = grouped // 2
    wblk = width // wsplit
    nloc = wblk // W
    direct = lands_in_place(nloc, msplit)
    lanes = vert_f32.shape[2]
    block_rows = cells * grouped
    groups = cell_groups(cells, grouped)
    group_cells = cells // groups
    group_rows = group_cells * grouped
    halves = 2
    half = width // halves
    kdev = kpt_ref.shape[1]
    all_cells = cell_ref.shape[1]
    mode_total = omega_ref.shape[1]
    disp = eig_ref.shape[1]

    chunks = [(g, h) for g in range(groups) for h in range(halves)]
    tiles_half = tiles // halves
    g_copies = {}

    def fetch(index):
        g, h = chunks[index]
        for cell in range(g * group_cells, (g + 1) * group_cells):
            for tile in range(h * tiles_half, (h + 1) * tiles_half):
                copy = pltpu.make_async_copy(
                    g_ref.at[cell, :, tile], g_buf.at[cell, tile], g_sem.at[cell, tile]
                )
                copy.start()
                g_copies[cell, tile] = copy

    small = []
    for at, (src, dst) in enumerate(
        [
            (eig_hbm, eig_ref), (omega_hbm, omega_ref), (q_hbm, q_ref),
            (phc_hbm, phc_ref), (kpt_hbm, kpt_ref), (cell_hbm, cell_ref),
        ]
    ):
        small.append(pltpu.make_async_copy(src, dst, small_sem.at[at]))
        small[-1].start()
    fetch(0)
    if len(chunks) > 1:
        fetch(1)

    barrier = pltpu.get_barrier_semaphore()
    pl.semaphore_signal(barrier, inc=1, device_id=(mate, ka), device_id_type=MESH)
    for step in range(1, nx):
        there = 2 * lax.rem(x + step, nx) + core
        pl.semaphore_signal(barrier, inc=1, device_id=(there, ka), device_id_type=MESH)
    for step in range(1, nka):
        there = lax.rem(ka + step, nka)
        pl.semaphore_signal(barrier, inc=1, device_id=(ph, there), device_id_type=MESH)

    for copy in small:
        copy.wait()
    spread_v = lax.broadcasted_iota(jnp.int32, (disp, 2 * disp), 0)
    spread_col = lax.broadcasted_iota(jnp.int32, (disp, 2 * disp), 1)
    even = (spread_col == 2 * spread_v).astype(jnp.float32)
    odd = (spread_col == 2 * spread_v + 1).astype(jnp.float32)

    def spread(values, pattern):
        return lax.dot_general(
            values, pattern, (((0,), (0,)), ((), ())),
            preferred_element_type=jnp.float32, precision=lax.Precision.HIGHEST,
        )

    real, imag = eig_ref[0], eig_ref[1]
    first = spread(real, even) - spread(imag, odd)
    second = spread(imag, even) + spread(real, odd)

    def by_owner(upper, lower):
        pieces = []
        for at in range(0, mode_total, modes):
            pieces += [upper[at : at + modes], lower[at : at + modes]]
        return jnp.concatenate(pieces, 0)

    scale = 1.0 / jnp.sqrt(2.0 * jnp.broadcast_to(omega_ref[...], (2 * disp, mode_total)).T)
    scale = by_owner(scale, scale)
    with_cos = by_owner(first, second)
    with_sin = by_owner(-second, first)
    numer = (
        q_ref[0] * phc_ref[0:1, :] + q_ref[1] * phc_ref[1:2, :] + q_ref[2] * phc_ref[2:3, :]
    )
    q_cos, q_sin = cos_sin(numer.astype(jnp.float32))
    pieces = []
    for p in range(phc_ref.shape[1]):
        pieces.append(
            (with_cos * q_cos[:, p : p + 1] + with_sin * q_sin[:, p : p + 1]) * scale
        )
    table[...] = jnp.concatenate(pieces, 1).astype(jnp.bfloat16)

    k_mine[...] = jnp.zeros_like(k_mine)
    k_mine[0:3, :] = kpt_ref[...].astype(jnp.float32)
    pl.semaphore_wait(barrier, nx + nka - 1)
    k_copies = []
    for step in range(1, ways):
        there = team * ways + lax.rem(spot + step, ways)
        copy = pltpu.make_async_remote_copy(
            src_ref=k_mine, dst_ref=k_all.at[spot],
            send_sem=k_ss.at[step], recv_sem=k_rs.at[spot],
            device_id=(ph, there), device_id_type=MESH,
        )
        copy.start()
        k_copies.append(copy)
    k_all[spot] = k_mine[...]

    def owned(owner, index):
        g, h = chunks[index]
        blocks = [
            part[cell, pl.ds(pl.multiple_of(owner * rows, 8), rows), h * half : (h + 1) * half]
            for cell in range(g * group_cells, (g + 1) * group_cells)
        ]
        return jnp.concatenate(
            [
                block[group * grouped : (group + 1) * grouped]
                for group in range(msplit)
                for block in blocks
            ],
            0,
        )

    def multiply(index):
        g, h = chunks[index]
        for cell in range(g * group_cells, (g + 1) * group_cells):
            for tile in range(h * tiles_half, (h + 1) * tiles_half, 2):
                g_copies[cell, tile].wait()
                g_copies[cell, tile + 1].wait()
                right = jnp.concatenate(
                    [
                        g_buf.at[cell, tile].reshape(depth, LANES)[...],
                        g_buf.at[cell, tile + 1].reshape(depth, LANES)[...],
                    ],
                    1,
                )
                part[cell, :, tile * LANES : (tile + 2) * LANES] = jnp.dot(
                    table[...], right, preferred_element_type=jnp.float32
                )

    core_copies, x_copies, v_copies = {}, {}, []

    def to_mate(index):
        for step in range(nx - 1, -1, -1):
            owner = 2 * lax.rem(x + step, nx) + (1 - core)
            core_send[index, step] = owned(owner, index).astype(jnp.bfloat16)
            copy = pltpu.make_async_remote_copy(
                src_ref=core_send.at[index, step], dst_ref=core_recv.at[index, step],
                send_sem=core_ss.at[index, step], recv_sem=core_rs.at[index, step],
                device_id=(mate, ka), device_id_type=MESH,
            )
            copy.start()
            core_copies[index, step] = copy

    def to_other_chips(index):
        for step in range(1, nx):
            owner = 2 * lax.rem(x + step, nx) + core
            core_copies[index, step].wait_recv()
            both = owned(owner, index) + core_recv[index, step].astype(jnp.float32)
            x_send[index, step - 1] = both.astype(jnp.bfloat16)
            copy = pltpu.make_async_remote_copy(
                src_ref=x_send.at[index, step - 1], dst_ref=x_recv.at[index, step - 1],
                send_sem=x_ss.at[index, step - 1], recv_sem=x_rs.at[index, step - 1],
                device_id=(owner, ka), device_id_type=MESH,
            )
            copy.start()
            x_copies[index, step] = copy

    def vertices(index):
        g, h = chunks[index]
        core_copies[index, 0].wait_recv()
        total = owned(ph, index) + core_recv[index, 0].astype(jnp.float32)
        for step in range(1, nx):
            x_copies[index, step].wait_recv()
            total = total + x_recv[index, step - 1].astype(jnp.float32)
        total = total.astype(jnp.bfloat16)
        here = wsplit // halves
        for group in range(msplit):
            for local in range(here):
                vert_send[group * wsplit + h * here + local, g] = total[
                    group * group_rows : (group + 1) * group_rows,
                    local * wblk : (local + 1) * wblk,
                ]
        for group in range(msplit):
            for local in range(here):
                block = group * wsplit + h * here + lax.rem(local + spot, here)
                for step in range(nka // ways - 1, -1, -1):
                    there = lax.rem(team + step, nka // ways) * ways + block

                    @pl.when(there != ka)
                    def _():
                        pltpu.make_async_remote_copy(
                            src_ref=vert_send.at[block, g], dst_ref=vert_recv.at[ka, g],
                            send_sem=v_ss.at[there, g], recv_sem=v_rs.at[ka, g],
                            device_id=(ph, there), device_id_type=MESH,
                        ).start()

                    @pl.when(there == ka)
                    def _():
                        vert_recv[ka, g] = vert_send[block, g]

    count = len(chunks)
    for index in range(count):
        multiply(index)
        if index + 2 < count:
            fetch(index + 2)
        to_mate(index)
        if index >= 1:
            to_other_chips(index - 1)
        if index >= 3:
            vertices(index - 3)
    to_other_chips(count - 1)
    for index in range(max(count - 3, 0), count - 1):
        vertices(index)

    for step in range(1, ways):
        src = lax.rem(spot + step, ways)
        pltpu.make_async_remote_copy(
            src_ref=k_mine, dst_ref=k_all.at[src],
            send_sem=k_ss.at[step], recv_sem=k_rs.at[src],
            device_id=(ph, team * ways + src), device_id_type=MESH,
        ).wait_recv()
    el_cells = jnp.concatenate(
        [cell_ref[...].astype(jnp.float32), jnp.zeros((5, all_cells), jnp.float32)], 0
    )

    def phases(src, carry):
        cosine, sine = cos_sin(
            lax.dot_general(
                el_cells, k_all[src], (((0,), (0,)), ((), ())), preferred_element_type=jnp.float32
            )
        )
        cos_re[src] = jnp.concatenate([cosine, -sine], 0).astype(jnp.bfloat16)
        cos_im[src] = jnp.concatenate([sine, cosine], 0).astype(jnp.bfloat16)
        return carry

    lax.fori_loop(0, ways, phases, 0)
    vertices(count - 1)

    for step in range(1, nka):
        src = lax.rem(ka + step, nka)
        for g in range(groups):
            pltpu.make_async_remote_copy(
                src_ref=vert_send.at[lax.rem(src, ways), g], dst_ref=vert_recv.at[src, g],
                send_sem=v_ss.at[src, g], recv_sem=v_rs.at[src, g],
                device_id=(ph, src), device_id_type=MESH,
            ).wait()
    for src in range(nka):
        for g in range(groups):
            at = src * block_rows + g * group_rows
            block = vert_recv[src, g].astype(jnp.float32)
            for tile in range(vert_f32.shape[0]):
                vert_f32[tile, at : at + group_rows, :] = block[:, tile * lanes : (tile + 1) * lanes]
    for mode in range(modes):
        for tile in range(vert_f32.shape[0]):
            re_rows = vert_f32[tile, pl.ds(mode, all_cells, stride=grouped), :]
            im_rows = vert_f32[tile, pl.ds(modes + mode, all_cells, stride=grouped), :]
            at = mode * wblk + tile * lanes
            turned[at : at + lanes, :] = (
                jnp.concatenate([re_rows, im_rows], 0).T.astype(jnp.bfloat16)
            )

    batch = 2 if modes % 2 == 0 else 1

    def strengths(step, carry):
        there = lax.rem(spot + step + 1, ways)
        phase_re, phase_im = cos_re[there], cos_im[there]
        for mode in range(0, modes, batch):
            left = turned[mode * wblk : (mode + batch) * wblk, :]
            bloch_re = jnp.dot(left, phase_re, preferred_element_type=jnp.float32)
            bloch_im = jnp.dot(left, phase_im, preferred_element_type=jnp.float32)
            squares = bloch_re * bloch_re + bloch_im * bloch_im
            summed = jnp.sum(squares.reshape(batch * nloc, W, kdev), axis=1) * (1.0 / normalizer)
            if direct:
                str_send[there, mode : mode + batch] = summed.reshape(batch, nloc, kdev)
            else:
                str_send[there, mode * nloc : (mode + batch) * nloc, :] = summed

        @pl.when(step < ways - 1)
        def _():
            strength_copy(there, there, spot).start()

        return carry

    def landing(src):
        if direct:
            return out_ref.at[:, pl.ds(pl.multiple_of(src * nloc, 8), nloc), :]
        return str_recv.at[src]

    def strength_copy(there, sem, src):
        return pltpu.make_async_remote_copy(
            src_ref=str_send.at[there], dst_ref=landing(src),
            send_sem=s_ss.at[sem], recv_sem=s_rs.at[src],
            device_id=(ph, team * ways + there), device_id_type=MESH,
        )

    lax.fori_loop(0, ways, strengths, 0)

    def place(src, held):
        group, piece = divmod(src, wsplit)
        for mode in range(modes):
            out_ref[group * modes + mode, piece * nloc : (piece + 1) * nloc, :] = held[
                src, mode * nloc : (mode + 1) * nloc, :
            ]

    if direct:
        own = pltpu.make_async_copy(str_send.at[spot], landing(spot), s_rs.at[spot])
        own.start()
    else:
        str_recv[spot] = str_send[spot]
    for step in range(1, ways):
        src = lax.rem(spot + step, ways)
        strength_copy(src, src, src).wait()
    if direct:
        own.wait()
    else:
        for src in range(ways):
            place(src, str_recv)
    for copy in list(core_copies.values()) + list(x_copies.values()) + k_copies:
        copy.wait_send()


def shards(g_wan, el_cells, ph_cells, q_point, kpoints, eigvec, omega):
    nph, nka = lax.axis_size("ph"), lax.axis_size("ka")
    cells, ph_loc, disp, parts, width = g_wan.shape
    tiles = width // LANES
    g_view = g_wan.reshape(cells, ph_loc * disp, parts, tiles, LANES).transpose(0, 1, 3, 2, 4)
    ways = team_size(nka)
    wsplit, msplit = splits(ways, width)
    mode_total = eigvec.shape[-1]
    modes = mode_total // nph
    kdev, all_cells = kpoints.shape[1], el_cells.shape[1]
    nx, wblk = nph // 2, width // wsplit
    nloc = wblk // W
    lanes = math.gcd(wblk, LANES)
    direct = lands_in_place(nloc, msplit)
    strength_block = (modes, nloc, kdev) if direct else (modes // msplit * nloc, kdev)
    mode_group = modes // msplit
    block_rows = cells * 2 * mode_group
    groups = cell_groups(cells, 2 * mode_group)
    group_rows = block_rows // groups
    chunks = groups * 2
    sent = (chunks, nx, msplit * group_rows, width // 2)
    passed = (chunks, nx - 1, msplit * group_rows, width // 2)
    bf16, f32 = jnp.bfloat16, jnp.float32
    vmem, dma = pltpu.VMEM, pltpu.SemaphoreType.DMA
    normalizer = float(all_cells * ph_loc * nph * W)
    return pl.pallas_call(
        functools.partial(kernel, nph, nka, normalizer),
        out_shape=jax.ShapeDtypeStruct((modes, W, kdev), f32),
        in_specs=[pl.BlockSpec(memory_space=pltpu.HBM)] * 7,
        out_specs=pl.BlockSpec(memory_space=pltpu.HBM if direct else vmem),
        scratch_shapes=[
            vmem(kpoints.shape, jnp.int32),
            vmem(el_cells.shape, jnp.int32),
            pltpu.SMEM(q_point.shape, jnp.int32),
            vmem(ph_cells.shape, jnp.int32),
            vmem(eigvec.shape, f32),
            vmem((1, mode_total), f32),
            dma((6,)),
            vmem((cells, tiles, ph_loc * disp, parts, LANES), bf16),
            vmem((2 * mode_total, ph_loc * disp * parts), bf16),
            vmem((cells, 2 * mode_total, width), f32),
            vmem(sent, bf16),
            vmem(sent, bf16),
            vmem(passed, bf16),
            vmem(passed, bf16),
            vmem((ways, groups, group_rows, wblk), bf16),
            vmem((nka, groups, group_rows, wblk), bf16),
            vmem((wblk // lanes, nka * block_rows, lanes), f32),
            vmem((mode_group * wblk, 2 * all_cells), bf16),
            vmem((8, kdev), f32),
            vmem((ways, 8, kdev), f32),
            vmem((ways, 2 * all_cells, kdev), bf16),
            vmem((ways, 2 * all_cells, kdev), bf16),
            vmem((ways, *strength_block), f32),
            vmem((8, LANES) if direct else (ways, *strength_block), f32),
            dma((cells, tiles)),
            dma(sent[:2]), dma(sent[:2]), dma(passed[:2]), dma(passed[:2]),
            dma((nka, groups)), dma((nka, groups)),
            dma((ways,)), dma((ways,)), dma((ways,)), dma((ways,)),
        ],
        compiler_params=pltpu.CompilerParams(
            collective_id=0, has_side_effects=True, vmem_limit_bytes=56 * 1024 * 1024
        ),
    )(g_view, kpoints, el_cells, q_point, ph_cells, eigvec, omega.reshape(1, mode_total))


def solution(mesh):
    return jax.shard_map(
        shards,
        mesh=mesh,
        in_specs=(
            P("ka", "ph", None, None, None),
            P(),
            P(None, "ph"),
            P(),
            P(None, "ka"),
            P(),
            P(),
        ),
        out_specs=P("ph", None, "ka"),
        check_vma=False,
    )
```

```python
import functools
import math

import jax
import jax.numpy as jnp
from jax import lax
from jax.experimental import pallas as pl
from jax.experimental.pallas import tpu as pltpu
from jax.sharding import PartitionSpec as P

W = 32
KGRID = 64
LANES = 128
MESH = pl.DeviceIdType.MESH


def team_size(nka):
    return nka


def splits(ways, width):
    by_width = math.gcd(ways, width // W)
    return by_width, ways // by_width


def cell_groups(cells, grouped):
    return 2 if cells % 2 == 0 and (cells // 2 * grouped) % 16 == 0 else 1


def padded(rows):
    return -(-rows // 16) * 16


def cos_sin(numerator):
    folded = numerator - KGRID * jnp.floor(numerator * (1.0 / KGRID))
    quarter = jnp.floor((folded + KGRID // 8) * (4.0 / KGRID))
    angle = (folded - quarter * (KGRID // 4)) * (2.0 * math.pi / KGRID)
    square = angle * angle
    cosine = 1.0 + square * (
        -1 / 2 + square * (1 / 24 + square * (-1 / 720 + square * (1 / 40320)))
    )
    sine = angle + angle * square * (
        -1 / 6 + square * (1 / 120 + square * (-1 / 5040 + square * (1 / 362880)))
    )
    odd = (quarter == 1.0) | (quarter == 3.0)
    cos_minus = (quarter == 1.0) | (quarter == 2.0)
    sin_minus = (quarter == 2.0) | (quarter == 3.0)
    cos_all = jnp.where(odd, sine, cosine)
    sin_all = jnp.where(odd, cosine, sine)
    return jnp.where(cos_minus, -cos_all, cos_all), jnp.where(sin_minus, -sin_all, sin_all)


def kernel(
    nph, nka, normalizer, g_ref, kpt_hbm, cell_hbm, q_hbm, phc_hbm, eig_hbm, omega_hbm, out_ref,
    kpt_ref, cell_ref, q_ref, phc_ref, eig_ref, omega_ref, small_sem,
    g_buf, table, part, core_send, core_recv, x_send, x_recv, vert_send, vert_recv, vert_f32, turned,
    k_mine, k_all, cos_re, cos_im, str_send, str_recv, str_f32, mean_send, mean_recv,
    g_sem, core_ss, core_rs, x_ss, x_rs, v_ss, v_rs, k_ss, k_rs, s_ss, s_rs, m_ss, m_rs,
):
    ph, ka = lax.axis_index("ph"), lax.axis_index("ka")
    nx = nph // 2
    core, x = lax.rem(ph, 2), lax.div(ph, 2)
    mate = 2 * x + (1 - core)
    cells, pairs, tiles = g_ref.shape[:3]
    depth = 2 * pairs
    width = tiles * LANES
    rows_all = part.shape[1]
    rows = rows_all // nph
    ways = team_size(nka)
    team, spot = lax.div(ka, ways), lax.rem(ka, ways)
    wsplit, msplit = splits(ways, width)
    grouped = rows // msplit
    modes = grouped // 2
    wblk = width // wsplit
    nloc = wblk // W
    str_rows = str_f32.shape[0]
    lanes = vert_f32.shape[2]
    block_rows = cells * grouped
    groups = cell_groups(cells, grouped)
    group_cells = cells // groups
    group_rows = group_cells * grouped
    halves = 2
    half = width // halves
    kdev = kpt_ref.shape[1]
    all_cells = cell_ref.shape[1]
    mode_total = omega_ref.shape[1]
    disp = eig_ref.shape[1]

    chunks = [(g, h) for g in range(groups) for h in range(halves)]
    tiles_half = tiles // halves
    g_copies = {}

    def fetch(index):
        g, h = chunks[index]
        for cell in range(g * group_cells, (g + 1) * group_cells):
            for tile in range(h * tiles_half, (h + 1) * tiles_half):
                copy = pltpu.make_async_copy(
                    g_ref.at[cell, :, tile], g_buf.at[cell, tile], g_sem.at[cell, tile]
                )
                copy.start()
                g_copies[cell, tile] = copy

    small = []
    for at, (src, dst) in enumerate(
        [
            (eig_hbm, eig_ref), (omega_hbm, omega_ref), (q_hbm, q_ref),
            (phc_hbm, phc_ref), (kpt_hbm, kpt_ref), (cell_hbm, cell_ref),
        ]
    ):
        small.append(pltpu.make_async_copy(src, dst, small_sem.at[at]))
        small[-1].start()
    fetch(0)
    if len(chunks) > 1:
        fetch(1)

    barrier = pltpu.get_barrier_semaphore()
    pl.semaphore_signal(barrier, inc=1, device_id=(mate, ka), device_id_type=MESH)
    for step in range(1, nx):
        there = 2 * lax.rem(x + step, nx) + core
        pl.semaphore_signal(barrier, inc=1, device_id=(there, ka), device_id_type=MESH)
    for step in range(1, nka):
        there = lax.rem(ka + step, nka)
        pl.semaphore_signal(barrier, inc=1, device_id=(ph, there), device_id_type=MESH)

    for copy in small:
        copy.wait()
    spread_v = lax.broadcasted_iota(jnp.int32, (disp, 2 * disp), 0)
    spread_col = lax.broadcasted_iota(jnp.int32, (disp, 2 * disp), 1)
    even = (spread_col == 2 * spread_v).astype(jnp.float32)
    odd = (spread_col == 2 * spread_v + 1).astype(jnp.float32)

    def spread(values, pattern):
        return lax.dot_general(
            values, pattern, (((0,), (0,)), ((), ())),
            preferred_element_type=jnp.float32, precision=lax.Precision.HIGHEST,
        )

    real, imag = eig_ref[0], eig_ref[1]
    first = spread(real, even) - spread(imag, odd)
    second = spread(imag, even) + spread(real, odd)

    def by_owner(upper, lower):
        pieces = []
        for at in range(0, mode_total, modes):
            pieces += [upper[at : at + modes], lower[at : at + modes]]
        return jnp.concatenate(pieces, 0)

    scale = 1.0 / jnp.sqrt(2.0 * jnp.broadcast_to(omega_ref[...], (2 * disp, mode_total)).T)
    scale = by_owner(scale, scale)
    with_cos = by_owner(first, second)
    with_sin = by_owner(-second, first)
    numer = (
        q_ref[0] * phc_ref[0:1, :] + q_ref[1] * phc_ref[1:2, :] + q_ref[2] * phc_ref[2:3, :]
    )
    q_cos, q_sin = cos_sin(numer.astype(jnp.float32))
    pieces = []
    for p in range(phc_ref.shape[1]):
        pieces.append(
            (with_cos * q_cos[:, p : p + 1] + with_sin * q_sin[:, p : p + 1]) * scale
        )
    table[...] = jnp.concatenate(pieces, 1).astype(jnp.bfloat16)

    k_mine[...] = jnp.zeros_like(k_mine)
    k_mine[0:3, :] = kpt_ref[...].astype(jnp.float32)
    pl.semaphore_wait(barrier, nx + nka - 1)
    k_copies = []
    for step in range(1, ways):
        there = team * ways + lax.rem(spot + step, ways)
        copy = pltpu.make_async_remote_copy(
            src_ref=k_mine, dst_ref=k_all.at[spot],
            send_sem=k_ss.at[step], recv_sem=k_rs.at[spot],
            device_id=(ph, there), device_id_type=MESH,
        )
        copy.start()
        k_copies.append(copy)
    k_all[spot] = k_mine[...]

    def owned(owner, index):
        g, h = chunks[index]
        blocks = [
            part[cell, pl.ds(pl.multiple_of(owner * rows, 8), rows), h * half : (h + 1) * half]
            for cell in range(g * group_cells, (g + 1) * group_cells)
        ]
        return jnp.concatenate(
            [
                block[group * grouped : (group + 1) * grouped]
                for group in range(msplit)
                for block in blocks
            ],
            0,
        )

    def multiply(index):
        g, h = chunks[index]
        for cell in range(g * group_cells, (g + 1) * group_cells):
            for tile in range(h * tiles_half, (h + 1) * tiles_half, 2):
                g_copies[cell, tile].wait()
                g_copies[cell, tile + 1].wait()
                right = jnp.concatenate(
                    [
                        g_buf.at[cell, tile].reshape(depth, LANES)[...],
                        g_buf.at[cell, tile + 1].reshape(depth, LANES)[...],
                    ],
                    1,
                )
                part[cell, :, tile * LANES : (tile + 2) * LANES] = jnp.dot(
                    table[...], right, preferred_element_type=jnp.float32
                )

    core_copies, x_copies, v_copies = {}, {}, []

    def to_mate(index):
        for step in range(nx - 1, -1, -1):
            owner = 2 * lax.rem(x + step, nx) + (1 - core)
            core_send[index, step] = owned(owner, index).astype(jnp.bfloat16)
            copy = pltpu.make_async_remote_copy(
                src_ref=core_send.at[index, step], dst_ref=core_recv.at[index, step],
                send_sem=core_ss.at[index, step], recv_sem=core_rs.at[index, step],
                device_id=(mate, ka), device_id_type=MESH,
            )
            copy.start()
            core_copies[index, step] = copy

    def to_other_chips(index):
        for step in range(1, nx):
            owner = 2 * lax.rem(x + step, nx) + core
            core_copies[index, step].wait_recv()
            both = owned(owner, index) + core_recv[index, step].astype(jnp.float32)
            x_send[index, step - 1] = both.astype(jnp.bfloat16)
            copy = pltpu.make_async_remote_copy(
                src_ref=x_send.at[index, step - 1], dst_ref=x_recv.at[index, step - 1],
                send_sem=x_ss.at[index, step - 1], recv_sem=x_rs.at[index, step - 1],
                device_id=(owner, ka), device_id_type=MESH,
            )
            copy.start()
            x_copies[index, step] = copy

    def vertices(index):
        g, h = chunks[index]
        core_copies[index, 0].wait_recv()
        total = owned(ph, index) + core_recv[index, 0].astype(jnp.float32)
        for step in range(1, nx):
            x_copies[index, step].wait_recv()
            total = total + x_recv[index, step - 1].astype(jnp.float32)
        total = total.astype(jnp.bfloat16)
        here = wsplit // halves
        for group in range(msplit):
            for local in range(here):
                vert_send[group * wsplit + h * here + local, g] = total[
                    group * group_rows : (group + 1) * group_rows,
                    local * wblk : (local + 1) * wblk,
                ]
        for group in range(msplit):
            for local in range(here):
                block = group * wsplit + h * here + lax.rem(local + spot, here)
                for step in range(nka // ways - 1, -1, -1):
                    there = lax.rem(team + step, nka // ways) * ways + block

                    @pl.when(there != ka)
                    def _():
                        pltpu.make_async_remote_copy(
                            src_ref=vert_send.at[block, g], dst_ref=vert_recv.at[ka, g],
                            send_sem=v_ss.at[there, g], recv_sem=v_rs.at[ka, g],
                            device_id=(ph, there), device_id_type=MESH,
                        ).start()

                    @pl.when(there == ka)
                    def _():
                        vert_recv[ka, g] = vert_send[block, g]

    count = len(chunks)
    for index in range(count):
        multiply(index)
        if index + 2 < count:
            fetch(index + 2)
        to_mate(index)
        if index >= 1:
            to_other_chips(index - 1)
        if index >= 3:
            vertices(index - 3)
    for index in range(max(count - 3, 0), count - 2):
        vertices(index)
    to_other_chips(count - 1)
    if count > 1:
        vertices(count - 2)

    for step in range(1, ways):
        src = lax.rem(spot + step, ways)
        pltpu.make_async_remote_copy(
            src_ref=k_mine, dst_ref=k_all.at[src],
            send_sem=k_ss.at[step], recv_sem=k_rs.at[src],
            device_id=(ph, team * ways + src), device_id_type=MESH,
        ).wait_recv()
    el_cells = jnp.concatenate(
        [cell_ref[...].astype(jnp.float32), jnp.zeros((5, all_cells), jnp.float32)], 0
    )

    def phases(src, carry):
        cosine, sine = cos_sin(
            lax.dot_general(
                el_cells, k_all[src], (((0,), (0,)), ((), ())), preferred_element_type=jnp.float32
            )
        )
        cos_re[src] = jnp.concatenate([cosine, -sine], 0).astype(jnp.bfloat16)
        cos_im[src] = jnp.concatenate([sine, cosine], 0).astype(jnp.bfloat16)
        return carry

    lax.fori_loop(0, ways, phases, 0)
    vertices(count - 1)

    for step in range(1, nka):
        src = lax.rem(ka + step, nka)
        for g in range(groups):
            pltpu.make_async_remote_copy(
                src_ref=vert_send.at[lax.rem(src, ways), g], dst_ref=vert_recv.at[src, g],
                send_sem=v_ss.at[src, g], recv_sem=v_rs.at[src, g],
                device_id=(ph, src), device_id_type=MESH,
            ).wait()
    for src in range(nka):
        for g in range(groups):
            at = src * block_rows + g * group_rows
            block = vert_recv[src, g].astype(jnp.float32)
            for tile in range(vert_f32.shape[0]):
                vert_f32[tile, at : at + group_rows, :] = block[:, tile * lanes : (tile + 1) * lanes]
    for mode in range(modes):
        for tile in range(vert_f32.shape[0]):
            re_rows = vert_f32[tile, pl.ds(mode, all_cells, stride=grouped), :]
            im_rows = vert_f32[tile, pl.ds(modes + mode, all_cells, stride=grouped), :]
            at = mode * wblk + tile * lanes
            turned[at : at + lanes, :] = (
                jnp.concatenate([re_rows, im_rows], 0).T.astype(jnp.bfloat16)
            )

    batch = 4 if modes % 4 == 0 else 1

    def strengths(step, carry):
        there = lax.rem(spot + step + 1, ways)
        phase_re, phase_im = cos_re[there], cos_im[there]
        for mode in range(0, modes, batch):
            left = turned[mode * wblk : (mode + batch) * wblk, :]
            bloch_re = jnp.dot(left, phase_re, preferred_element_type=jnp.float32)
            bloch_im = jnp.dot(left, phase_im, preferred_element_type=jnp.float32)
            squares = bloch_re * bloch_re + bloch_im * bloch_im
            summed = jnp.sum(squares.reshape(batch * nloc, W, kdev), axis=1) * (1.0 / normalizer)
            str_f32[mode * nloc : (mode + batch) * nloc, :] = summed
        held = str_f32[...]
        mean = jnp.sum(held, axis=1, keepdims=True) * (1.0 / kdev)
        str_send[there] = (held - mean).astype(jnp.bfloat16)
        mean_send[there, :, 0:str_rows] = jnp.broadcast_to(mean, (str_rows, LANES)).T[0:1, :]

        @pl.when(step < ways - 1)
        def _():
            for copy in strength_copies(there, spot):
                copy.start()

        return carry

    def strength_copies(there, src):
        return [
            pltpu.make_async_remote_copy(
                src_ref=outgoing.at[there], dst_ref=incoming.at[src],
                send_sem=sent.at[there], recv_sem=got.at[src],
                device_id=(ph, team * ways + there), device_id_type=MESH,
            )
            for outgoing, incoming, sent, got in (
                (mean_send, mean_recv, m_ss, m_rs), (str_send, str_recv, s_ss, s_rs)
            )
        ]

    str_f32[...] = jnp.zeros_like(str_f32)
    mean_send[...] = jnp.zeros_like(mean_send)
    lax.fori_loop(0, ways, strengths, 0)

    def place(src):
        row = mean_recv[src][:, 0:str_rows]
        mean = jnp.broadcast_to(row, (LANES, str_rows)).T[:, 0:1]
        held = str_recv[src].astype(jnp.float32) + mean
        group, piece = divmod(src, wsplit)
        for mode in range(modes):
            out_ref[group * modes + mode, piece * nloc : (piece + 1) * nloc, :] = held[
                mode * nloc : (mode + 1) * nloc, :
            ]

    str_recv[spot] = str_send[spot]
    mean_recv[spot] = mean_send[spot]
    for step in range(1, ways):
        src = lax.rem(spot + step, ways)
        for copy in strength_copies(src, src):
            copy.wait()
    for src in range(ways):
        place(src)
    for copy in list(core_copies.values()) + list(x_copies.values()) + k_copies:
        copy.wait_send()


def shards(g_wan, el_cells, ph_cells, q_point, kpoints, eigvec, omega):
    nph, nka = lax.axis_size("ph"), lax.axis_size("ka")
    cells, ph_loc, disp, parts, width = g_wan.shape
    tiles = width // LANES
    g_view = g_wan.reshape(cells, ph_loc * disp, parts, tiles, LANES).transpose(0, 1, 3, 2, 4)
    ways = team_size(nka)
    wsplit, msplit = splits(ways, width)
    mode_total = eigvec.shape[-1]
    modes = mode_total // nph
    kdev, all_cells = kpoints.shape[1], el_cells.shape[1]
    nx, wblk = nph // 2, width // wsplit
    nloc = wblk // W
    lanes = math.gcd(wblk, LANES)
    str_rows = padded(modes // msplit * nloc)
    mean_lanes = -(-str_rows // LANES) * LANES
    mode_group = modes // msplit
    block_rows = cells * 2 * mode_group
    groups = cell_groups(cells, 2 * mode_group)
    group_rows = block_rows // groups
    chunks = groups * 2
    sent = (chunks, nx, msplit * group_rows, width // 2)
    passed = (chunks, nx - 1, msplit * group_rows, width // 2)
    bf16, f32 = jnp.bfloat16, jnp.float32
    vmem, dma = pltpu.VMEM, pltpu.SemaphoreType.DMA
    normalizer = float(all_cells * ph_loc * nph * W)
    return pl.pallas_call(
        functools.partial(kernel, nph, nka, normalizer),
        out_shape=jax.ShapeDtypeStruct((modes, W, kdev), f32),
        in_specs=[pl.BlockSpec(memory_space=pltpu.HBM)] * 7,
        out_specs=pl.BlockSpec(memory_space=vmem),
        scratch_shapes=[
            vmem(kpoints.shape, jnp.int32),
            vmem(el_cells.shape, jnp.int32),
            pltpu.SMEM(q_point.shape, jnp.int32),
            vmem(ph_cells.shape, jnp.int32),
            vmem(eigvec.shape, f32),
            vmem((1, mode_total), f32),
            dma((6,)),
            vmem((cells, tiles, ph_loc * disp, parts, LANES), bf16),
            vmem((2 * mode_total, ph_loc * disp * parts), bf16),
            vmem((cells, 2 * mode_total, width), f32),
            vmem(sent, bf16),
            vmem(sent, bf16),
            vmem(passed, bf16),
            vmem(passed, bf16),
            vmem((ways, groups, group_rows, wblk), bf16),
            vmem((nka, groups, group_rows, wblk), bf16),
            vmem((wblk // lanes, nka * block_rows, lanes), f32),
            vmem((mode_group * wblk, 2 * all_cells), bf16),
            vmem((8, kdev), f32),
            vmem((ways, 8, kdev), f32),
            vmem((ways, 2 * all_cells, kdev), bf16),
            vmem((ways, 2 * all_cells, kdev), bf16),
            vmem((ways, str_rows, kdev), bf16),
            vmem((ways, str_rows, kdev), bf16),
            vmem((str_rows, kdev), f32),
            vmem((ways, 1, mean_lanes), f32),
            vmem((ways, 1, mean_lanes), f32),
            dma((cells, tiles)),
            dma(sent[:2]), dma(sent[:2]), dma(passed[:2]), dma(passed[:2]),
            dma((nka, groups)), dma((nka, groups)),
            dma((ways,)), dma((ways,)), dma((ways,)), dma((ways,)), dma((ways,)), dma((ways,)),
        ],
        compiler_params=pltpu.CompilerParams(
            collective_id=0, has_side_effects=True, vmem_limit_bytes=56 * 1024 * 1024
        ),
    )(g_view, kpoints, el_cells, q_point, ph_cells, eigvec, omega.reshape(1, mode_total))


def solution(mesh):
    return jax.shard_map(
        shards,
        mesh=mesh,
        in_specs=(
            P("ka", "ph", None, None, None),
            P(),
            P(None, "ph"),
            P(),
            P(None, "ka"),
            P(),
            P(),
        ),
        out_specs=P("ph", None, "ka"),
        check_vma=False,
    )
```

```python
import functools
import math

import jax
import jax.numpy as jnp
from jax import lax
from jax.experimental import pallas as pl
from jax.experimental.pallas import tpu as pltpu
from jax.sharding import PartitionSpec as P

W = 32
KGRID = 64
LANES = 128
MESH = pl.DeviceIdType.MESH


def team_size(nka):
    return nka


def splits(ways, width):
    by_width = math.gcd(ways, width // W)
    return by_width, ways // by_width


def cell_groups(cells, grouped):
    return 2 if cells % 2 == 0 and (cells // 2 * grouped) % 16 == 0 else 1


def padded(rows):
    return -(-rows // 16) * 16


def cos_sin(numerator):
    folded = numerator - KGRID * jnp.floor(numerator * (1.0 / KGRID))
    quarter = jnp.floor((folded + KGRID // 8) * (4.0 / KGRID))
    angle = (folded - quarter * (KGRID // 4)) * (2.0 * math.pi / KGRID)
    square = angle * angle
    cosine = 1.0 + square * (
        -1 / 2 + square * (1 / 24 + square * (-1 / 720 + square * (1 / 40320)))
    )
    sine = angle + angle * square * (
        -1 / 6 + square * (1 / 120 + square * (-1 / 5040 + square * (1 / 362880)))
    )
    odd = (quarter == 1.0) | (quarter == 3.0)
    cos_minus = (quarter == 1.0) | (quarter == 2.0)
    sin_minus = (quarter == 2.0) | (quarter == 3.0)
    cos_all = jnp.where(odd, sine, cosine)
    sin_all = jnp.where(odd, cosine, sine)
    return jnp.where(cos_minus, -cos_all, cos_all), jnp.where(sin_minus, -sin_all, sin_all)


def kernel(
    nph, nka, normalizer, g_ref, kpt_hbm, cell_hbm, q_hbm, phc_hbm, eig_hbm, omega_hbm, out_ref,
    kpt_ref, cell_ref, q_ref, phc_ref, eig_ref, omega_ref, small_sem,
    g_buf, table, part, core_send, core_recv, x_send, x_recv, vert_send, vert_recv, vert_f32, turned,
    k_mine, k_all, cos_re, cos_im, str_send, str_recv, str_f32, mean_send, mean_recv,
    g_sem, core_ss, core_rs, x_ss, x_rs, v_ss, v_rs, k_ss, k_rs, s_ss, s_rs, m_ss, m_rs,
):
    ph, ka = lax.axis_index("ph"), lax.axis_index("ka")
    nx = nph // 2
    core, x = lax.rem(ph, 2), lax.div(ph, 2)
    mate = 2 * x + (1 - core)
    cells, pairs, tiles = g_ref.shape[:3]
    depth = 2 * pairs
    width = tiles * LANES
    rows_all = part.shape[1]
    rows = rows_all // nph
    ways = team_size(nka)
    team, spot = lax.div(ka, ways), lax.rem(ka, ways)
    wsplit, msplit = splits(ways, width)
    grouped = rows // msplit
    modes = grouped // 2
    wblk = width // wsplit
    nloc = wblk // W
    str_rows = str_f32.shape[0]
    lanes = vert_f32.shape[2]
    block_rows = cells * grouped
    groups = cell_groups(cells, grouped)
    group_cells = cells // groups
    group_rows = group_cells * grouped
    halves = 2
    half = width // halves
    kdev = kpt_ref.shape[1]
    all_cells = cell_ref.shape[1]
    mode_total = omega_ref.shape[1]
    disp = eig_ref.shape[1]

    chunks = [(g, h) for g in range(groups) for h in range(halves)]
    tiles_half = tiles // halves
    g_copies = {}

    def fetch(index):
        g, h = chunks[index]
        for cell in range(g * group_cells, (g + 1) * group_cells):
            for tile in range(h * tiles_half, (h + 1) * tiles_half):
                copy = pltpu.make_async_copy(
                    g_ref.at[cell, :, tile], g_buf.at[cell, tile], g_sem.at[cell, tile]
                )
                copy.start()
                g_copies[cell, tile] = copy

    small = []
    for at, (src, dst) in enumerate(
        [
            (eig_hbm, eig_ref), (omega_hbm, omega_ref), (q_hbm, q_ref),
            (phc_hbm, phc_ref), (kpt_hbm, kpt_ref), (cell_hbm, cell_ref),
        ]
    ):
        small.append(pltpu.make_async_copy(src, dst, small_sem.at[at]))
        small[-1].start()
    fetch(0)
    if len(chunks) > 1:
        fetch(1)

    barrier = pltpu.get_barrier_semaphore()
    pl.semaphore_signal(barrier, inc=1, device_id=(mate, ka), device_id_type=MESH)
    for step in range(1, nx):
        there = 2 * lax.rem(x + step, nx) + core
        pl.semaphore_signal(barrier, inc=1, device_id=(there, ka), device_id_type=MESH)
    for step in range(1, nka):
        there = lax.rem(ka + step, nka)
        pl.semaphore_signal(barrier, inc=1, device_id=(ph, there), device_id_type=MESH)

    for copy in small:
        copy.wait()
    spread_v = lax.broadcasted_iota(jnp.int32, (disp, 2 * disp), 0)
    spread_col = lax.broadcasted_iota(jnp.int32, (disp, 2 * disp), 1)
    even = (spread_col == 2 * spread_v).astype(jnp.float32)
    odd = (spread_col == 2 * spread_v + 1).astype(jnp.float32)

    def spread(values, pattern):
        return lax.dot_general(
            values, pattern, (((0,), (0,)), ((), ())),
            preferred_element_type=jnp.float32, precision=lax.Precision.HIGHEST,
        )

    real, imag = eig_ref[0], eig_ref[1]
    first = spread(real, even) - spread(imag, odd)
    second = spread(imag, even) + spread(real, odd)

    def by_owner(upper, lower):
        pieces = []
        for at in range(0, mode_total, modes):
            pieces += [upper[at : at + modes], lower[at : at + modes]]
        return jnp.concatenate(pieces, 0)

    scale = 1.0 / jnp.sqrt(2.0 * jnp.broadcast_to(omega_ref[...], (2 * disp, mode_total)).T)
    scale = by_owner(scale, scale)
    with_cos = by_owner(first, second)
    with_sin = by_owner(-second, first)
    numer = (
        q_ref[0] * phc_ref[0:1, :] + q_ref[1] * phc_ref[1:2, :] + q_ref[2] * phc_ref[2:3, :]
    )
    q_cos, q_sin = cos_sin(numer.astype(jnp.float32))
    pieces = []
    for p in range(phc_ref.shape[1]):
        pieces.append(
            (with_cos * q_cos[:, p : p + 1] + with_sin * q_sin[:, p : p + 1]) * scale
        )
    table[...] = jnp.concatenate(pieces, 1).astype(jnp.bfloat16)

    k_mine[...] = jnp.zeros_like(k_mine)
    k_mine[0:3, :] = kpt_ref[...].astype(jnp.float32)
    pl.semaphore_wait(barrier, nx + nka - 1)
    k_copies = []
    for step in range(1, ways):
        there = team * ways + lax.rem(spot + step, ways)
        copy = pltpu.make_async_remote_copy(
            src_ref=k_mine, dst_ref=k_all.at[spot],
            send_sem=k_ss.at[step], recv_sem=k_rs.at[spot],
            device_id=(ph, there), device_id_type=MESH,
        )
        copy.start()
        k_copies.append(copy)
    k_all[spot] = k_mine[...]

    def owned(owner, index):
        g, h = chunks[index]
        blocks = [
            part[cell, pl.ds(pl.multiple_of(owner * rows, 8), rows), h * half : (h + 1) * half]
            for cell in range(g * group_cells, (g + 1) * group_cells)
        ]
        return jnp.concatenate(
            [
                block[group * grouped : (group + 1) * grouped]
                for group in range(msplit)
                for block in blocks
            ],
            0,
        )

    def multiply(index):
        g, h = chunks[index]
        for cell in range(g * group_cells, (g + 1) * group_cells):
            for tile in range(h * tiles_half, (h + 1) * tiles_half, 2):
                g_copies[cell, tile].wait()
                g_copies[cell, tile + 1].wait()
                right = jnp.concatenate(
                    [
                        g_buf.at[cell, tile].reshape(depth, LANES)[...],
                        g_buf.at[cell, tile + 1].reshape(depth, LANES)[...],
                    ],
                    1,
                )
                part[cell, :, tile * LANES : (tile + 2) * LANES] = jnp.dot(
                    table[...], right, preferred_element_type=jnp.float32
                )

    core_copies, x_copies, v_copies = {}, {}, []

    def to_mate(index):
        for step in range(nx - 1, -1, -1):
            owner = 2 * lax.rem(x + step, nx) + (1 - core)
            core_send[index, step] = owned(owner, index).astype(jnp.bfloat16)
            copy = pltpu.make_async_remote_copy(
                src_ref=core_send.at[index, step], dst_ref=core_recv.at[index, step],
                send_sem=core_ss.at[index, step], recv_sem=core_rs.at[index, step],
                device_id=(mate, ka), device_id_type=MESH,
            )
            copy.start()
            core_copies[index, step] = copy

    def to_other_chips(index):
        for step in range(1, nx):
            owner = 2 * lax.rem(x + step, nx) + core
            core_copies[index, step].wait_recv()
            both = owned(owner, index) + core_recv[index, step].astype(jnp.float32)
            x_send[index, step - 1] = both.astype(jnp.bfloat16)
            copy = pltpu.make_async_remote_copy(
                src_ref=x_send.at[index, step - 1], dst_ref=x_recv.at[index, step - 1],
                send_sem=x_ss.at[index, step - 1], recv_sem=x_rs.at[index, step - 1],
                device_id=(owner, ka), device_id_type=MESH,
            )
            copy.start()
            x_copies[index, step] = copy

    def vertices(index):
        g, h = chunks[index]
        core_copies[index, 0].wait_recv()
        total = owned(ph, index) + core_recv[index, 0].astype(jnp.float32)
        for step in range(1, nx):
            x_copies[index, step].wait_recv()
            total = total + x_recv[index, step - 1].astype(jnp.float32)
        total = total.astype(jnp.bfloat16)
        here = wsplit // halves
        for group in range(msplit):
            for local in range(here):
                vert_send[group * wsplit + h * here + local, g] = total[
                    group * group_rows : (group + 1) * group_rows,
                    local * wblk : (local + 1) * wblk,
                ]
        for group in range(msplit):
            for local in range(here):
                block = group * wsplit + h * here + lax.rem(local + spot, here)
                for step in range(nka // ways - 1, -1, -1):
                    there = lax.rem(team + step, nka // ways) * ways + block

                    @pl.when(there != ka)
                    def _():
                        pltpu.make_async_remote_copy(
                            src_ref=vert_send.at[block, g], dst_ref=vert_recv.at[ka, g],
                            send_sem=v_ss.at[there, g], recv_sem=v_rs.at[ka, g],
                            device_id=(ph, there), device_id_type=MESH,
                        ).start()

                    @pl.when(there == ka)
                    def _():
                        vert_recv[ka, g] = vert_send[block, g]

    count = len(chunks)
    for index in range(count):
        multiply(index)
        if index + 2 < count:
            fetch(index + 2)
        to_mate(index)
        if index >= 1:
            to_other_chips(index - 1)
        if index >= 3:
            vertices(index - 3)
    for index in range(max(count - 3, 0), count - 2):
        vertices(index)
    to_other_chips(count - 1)
    if count > 1:
        vertices(count - 2)

    for step in range(1, ways):
        src = lax.rem(spot + step, ways)
        pltpu.make_async_remote_copy(
            src_ref=k_mine, dst_ref=k_all.at[src],
            send_sem=k_ss.at[step], recv_sem=k_rs.at[src],
            device_id=(ph, team * ways + src), device_id_type=MESH,
        ).wait_recv()
    el_cells = jnp.concatenate(
        [cell_ref[...].astype(jnp.float32), jnp.zeros((5, all_cells), jnp.float32)], 0
    )

    def phases(src, carry):
        cosine, sine = cos_sin(
            lax.dot_general(
                el_cells, k_all[src], (((0,), (0,)), ((), ())), preferred_element_type=jnp.float32
            )
        )
        cos_re[src] = jnp.concatenate([cosine, -sine], 0).astype(jnp.bfloat16)
        cos_im[src] = jnp.concatenate([sine, cosine], 0).astype(jnp.bfloat16)
        return carry

    lax.fori_loop(0, ways, phases, 0)
    vertices(count - 1)

    for src in range(nka):
        for g in range(groups):

            @pl.when(src != ka)
            def _():
                pltpu.make_async_remote_copy(
                    src_ref=vert_send.at[src % ways, g], dst_ref=vert_recv.at[src, g],
                    send_sem=v_ss.at[src, g], recv_sem=v_rs.at[src, g],
                    device_id=(ph, src), device_id_type=MESH,
                ).wait()

            at = src * block_rows + g * group_rows
            block = vert_recv[src, g].astype(jnp.float32)
            for tile in range(vert_f32.shape[0]):
                vert_f32[tile, at : at + group_rows, :] = block[:, tile * lanes : (tile + 1) * lanes]
    for mode in range(modes):
        for tile in range(vert_f32.shape[0]):
            re_rows = vert_f32[tile, pl.ds(mode, all_cells, stride=grouped), :]
            im_rows = vert_f32[tile, pl.ds(modes + mode, all_cells, stride=grouped), :]
            at = mode * wblk + tile * lanes
            turned[at : at + lanes, :] = (
                jnp.concatenate([re_rows, im_rows], 0).T.astype(jnp.bfloat16)
            )

    batch = 4 if modes % 4 == 0 else 1

    def strengths(step, carry):
        reach = lax.div(step + 1, 2)
        there = lax.rem(spot + ways // 2 + reach - 2 * reach * lax.rem(step, 2), ways)
        phase_re, phase_im = cos_re[there], cos_im[there]
        for mode in range(0, modes, batch):
            left = turned[mode * wblk : (mode + batch) * wblk, :]
            bloch_re = jnp.dot(left, phase_re, preferred_element_type=jnp.float32)
            bloch_im = jnp.dot(left, phase_im, preferred_element_type=jnp.float32)
            squares = bloch_re * bloch_re + bloch_im * bloch_im
            summed = jnp.sum(squares.reshape(batch * nloc, W, kdev), axis=1) * (1.0 / normalizer)
            str_f32[mode * nloc : (mode + batch) * nloc, :] = summed
        held = str_f32[...]
        mean = jnp.sum(held, axis=1, keepdims=True) * (1.0 / kdev)
        str_send[there] = (held - mean).astype(jnp.bfloat16)
        mean_send[there, :, 0:str_rows] = jnp.broadcast_to(mean, (str_rows, LANES)).T[0:1, :]

        @pl.when(there != spot)
        def _():
            for copy in strength_copies(there, spot):
                copy.start()

        return carry

    def strength_copies(there, src):
        return [
            pltpu.make_async_remote_copy(
                src_ref=outgoing.at[there], dst_ref=incoming.at[src],
                send_sem=sent.at[there], recv_sem=got.at[src],
                device_id=(ph, team * ways + there), device_id_type=MESH,
            )
            for outgoing, incoming, sent, got in (
                (mean_send, mean_recv, m_ss, m_rs), (str_send, str_recv, s_ss, s_rs)
            )
        ]

    str_f32[...] = jnp.zeros_like(str_f32)
    mean_send[...] = jnp.zeros_like(mean_send)
    lax.fori_loop(0, ways, strengths, 0)

    def place(src):
        row = mean_recv[src][:, 0:str_rows]
        mean = jnp.broadcast_to(row, (LANES, str_rows)).T[:, 0:1]
        held = str_recv[src].astype(jnp.float32) + mean
        group, piece = divmod(src, wsplit)
        for mode in range(modes):
            out_ref[group * modes + mode, piece * nloc : (piece + 1) * nloc, :] = held[
                mode * nloc : (mode + 1) * nloc, :
            ]

    str_recv[spot] = str_send[spot]
    mean_recv[spot] = mean_send[spot]
    for src in range(ways):

        @pl.when(src != spot)
        def _():
            for copy in strength_copies(src, src):
                copy.wait()

        place(src)
    for copy in list(core_copies.values()) + list(x_copies.values()) + k_copies:
        copy.wait_send()


def shards(g_wan, el_cells, ph_cells, q_point, kpoints, eigvec, omega):
    nph, nka = lax.axis_size("ph"), lax.axis_size("ka")
    cells, ph_loc, disp, parts, width = g_wan.shape
    tiles = width // LANES
    g_view = g_wan.reshape(cells, ph_loc * disp, parts, tiles, LANES).transpose(0, 1, 3, 2, 4)
    ways = team_size(nka)
    wsplit, msplit = splits(ways, width)
    mode_total = eigvec.shape[-1]
    modes = mode_total // nph
    kdev, all_cells = kpoints.shape[1], el_cells.shape[1]
    nx, wblk = nph // 2, width // wsplit
    nloc = wblk // W
    lanes = math.gcd(wblk, LANES)
    str_rows = padded(modes // msplit * nloc)
    mean_lanes = -(-str_rows // LANES) * LANES
    mode_group = modes // msplit
    block_rows = cells * 2 * mode_group
    groups = cell_groups(cells, 2 * mode_group)
    group_rows = block_rows // groups
    chunks = groups * 2
    sent = (chunks, nx, msplit * group_rows, width // 2)
    passed = (chunks, nx - 1, msplit * group_rows, width // 2)
    bf16, f32 = jnp.bfloat16, jnp.float32
    vmem, dma = pltpu.VMEM, pltpu.SemaphoreType.DMA
    normalizer = float(all_cells * ph_loc * nph * W)
    return pl.pallas_call(
        functools.partial(kernel, nph, nka, normalizer),
        out_shape=jax.ShapeDtypeStruct((modes, W, kdev), f32),
        in_specs=[pl.BlockSpec(memory_space=pltpu.HBM)] * 7,
        out_specs=pl.BlockSpec(memory_space=vmem),
        scratch_shapes=[
            vmem(kpoints.shape, jnp.int32),
            vmem(el_cells.shape, jnp.int32),
            pltpu.SMEM(q_point.shape, jnp.int32),
            vmem(ph_cells.shape, jnp.int32),
            vmem(eigvec.shape, f32),
            vmem((1, mode_total), f32),
            dma((6,)),
            vmem((cells, tiles, ph_loc * disp, parts, LANES), bf16),
            vmem((2 * mode_total, ph_loc * disp * parts), bf16),
            vmem((cells, 2 * mode_total, width), f32),
            vmem(sent, bf16),
            vmem(sent, bf16),
            vmem(passed, bf16),
            vmem(passed, bf16),
            vmem((ways, groups, group_rows, wblk), bf16),
            vmem((nka, groups, group_rows, wblk), bf16),
            vmem((wblk // lanes, nka * block_rows, lanes), f32),
            vmem((mode_group * wblk, 2 * all_cells), bf16),
            vmem((8, kdev), f32),
            vmem((ways, 8, kdev), f32),
            vmem((ways, 2 * all_cells, kdev), bf16),
            vmem((ways, 2 * all_cells, kdev), bf16),
            vmem((ways, str_rows, kdev), bf16),
            vmem((ways, str_rows, kdev), bf16),
            vmem((str_rows, kdev), f32),
            vmem((ways, 1, mean_lanes), f32),
            vmem((ways, 1, mean_lanes), f32),
            dma((cells, tiles)),
            dma(sent[:2]), dma(sent[:2]), dma(passed[:2]), dma(passed[:2]),
            dma((nka, groups)), dma((nka, groups)),
            dma((ways,)), dma((ways,)), dma((ways,)), dma((ways,)), dma((ways,)), dma((ways,)),
        ],
        compiler_params=pltpu.CompilerParams(
            collective_id=0, has_side_effects=True, vmem_limit_bytes=56 * 1024 * 1024
        ),
    )(g_view, kpoints, el_cells, q_point, ph_cells, eigvec, omega.reshape(1, mode_total))


def solution(mesh):
    return jax.shard_map(
        shards,
        mesh=mesh,
        in_specs=(
            P("ka", "ph", None, None, None),
            P(),
            P(None, "ph"),
            P(),
            P(None, "ka"),
            P(),
            P(),
        ),
        out_specs=P("ph", None, "ka"),
        check_vma=False,
    )
```
